32 devices in a mesh: groups: 2 (over y), wide: 4 (over z), lev: 2 (over x), fld: 2 (over core).
Axes of the slice: x: 2, y: 2, z: 4, core: 2. Of those that a mesh axis runs over, the one named last changes fastest.
Arguments:
- grid_state: bfloat16 [4, 3, 8, 512, 1024], P(('groups', 'fld'), None, 'lev', 'wide'), parts along dimension 0, may hold values from -6 to 6
- wave_slots: int32 [512], replicated, may hold values from 0 to 511, each once
- lat_basis: bfloat16 [512, 512, 512], P(('wide', 'lev')), may hold values from -0.25 to 0.25
- vert_modes: float32 [8, 8], replicated, may hold values from -1 to 1, as said below
- vert_rates: float32 [3, 8], replicated, may hold values from 0.05 to 20
- band_sizes: int32 [16], replicated, may hold values from 1 to 64, 512 in all
- norm_gain: float32 [24], replicated, may hold values from 0.25 to 1.75
- w_in: bfloat16 [512, 24], replicated, may hold values from -1.25 to 1.25
- band_bias: float32 [512, 16], replicated, may hold values from -6 to 6
- w_mid: bfloat16 [512, 512], replicated, may hold values from -0.25 to 0.25
- w_out: bfloat16 [24, 512], replicated, may hold values from -0.25 to 0.25
Outputs:
- spectral: float32 [512, 4, 3, 8, 2, 512], P(('wide', 'lev'), ('groups', 'fld')), parts along dimension 1
- new_state: bfloat16 [4, 3, 8, 512, 1024], P(('groups', 'fld'), None, None, ('wide', 'lev')), parts along dimension 0
The draws below stay inside these ranges and needn't reach their ends.
There are 2 independent parts, one for each index of `groups`. The reference program is written for one: setup_inputs(seed, part) draws one part's arguments, and reference() takes and returns one part's arrays. A program takes and returns all parts, laid end to end along the dimension named above; an argument that names none is the same for every part. Nothing has to cross between parts.
Inputs may be any that keep to these rules, and one draw needn't show every extreme that they name: `wave_slots`: each number of 0 to 511 stands in exactly one slot. `band_sizes`: the 16 sizes sum to 512. `vert_modes`: an orthonormal matrix.
All inputs are finite; a program needn't handle non-finite values.
Results may differ from the reference program's by a relative error of at most 0.011.
Values may be sent and summed in bfloat16 or wider, within the bound.
No kernel may reach another device: no remote copies, remote signals or barrier semaphores. Data moves between devices by JAX's collectives and lax.ppermute only.
A program may use at most 192 MiB of HBM per device.

```python
import math
import jax
import jax.numpy as jnp
import numpy as np
from jax import lax

M = 512
NLAT = 512
NLON = 1024
FIELD_COUNT = 3
UNITS = 512
BANDS = 16
BAND_MOST = 64
LEVELS = 8
ENSEMBLE_SIZE = 2
FEAT = 24


def draw_vert_modes(key, part):
    raw_matrix = jax.random.normal(jax.random.fold_in(key, 11), (LEVELS, LEVELS), jnp.float32)
    orthonormal, upper_tri = jnp.linalg.qr(raw_matrix)
    return orthonormal.astype(jnp.float32)


def block_levels(own_key, extent, split, smallest, largest):
    def one(position, shards_of):
        heights = jax.random.uniform(jax.random.fold_in(jax.random.fold_in(own_key, 6), position), (shards_of,), jnp.float32, smallest / len(split), largest / len(split))
        return jnp.repeat(jnp.exp(heights), extent[position] // shards_of).reshape((-1,) + (1,) * (len(extent) - position - 1))

    level = one(*split[0])
    for cut in split[1:]:
        level = level * one(*cut)
    return level


def split_up(number_of, total, bound, slope):
    weights = [(1 << 20) // math.isqrt(standing ** slope) + 1 for standing in range(2, number_of + 1)]
    rest, holding = total - bound - (number_of - 1), [1] * (number_of - 1)
    while rest > 0:
        candidates = [i for i in range(number_of - 1) if holding[i] < bound]
        whole, budget = sum([weights[i] for i in candidates]), rest
        for i in candidates:
            extra = min(bound - holding[i], max(1, budget * weights[i] // whole), rest)
            holding[i] = holding[i] + extra
            rest = rest - extra
    return np.array([bound] + holding)


def ragged(stream_key, amount, total, bound, slope):
    if amount == 2:
        one = jax.random.randint(stream_key, (), max(1, total - bound), min(bound, total - 1) + 1)
        return jnp.stack([one, total - one])
    lengths = jnp.asarray(split_up(amount, total, bound, slope), jnp.int32)
    pairs = (amount - 1) // 2
    giver, taker = lengths[1:1 + 2 * pairs:2], lengths[2:2 + 2 * pairs:2]
    margin = jnp.minimum(giver - 1, bound - taker)
    passed = jax.random.randint(jax.random.fold_in(stream_key, 1), (pairs,), 0, 1 << 20) % (margin + 1)
    lengths = lengths.at[1:1 + 2 * pairs:2].set(giver - passed).at[2:2 + 2 * pairs:2].set(taker + passed)
    return lengths[jax.random.permutation(jax.random.fold_in(stream_key, 2), amount)]


def centred(own_key, shape, spread, reach, split=(), held_as=jnp.bfloat16):
    drawn = spread * jax.random.normal(own_key, shape, jnp.float32)
    if split:
        drawn = drawn * block_levels(own_key, shape, split, -0.22, 0.18)
    return jnp.clip(drawn, -reach, reach).astype(held_as)


def setup_inputs(seed: int = 0, part: int = 0) -> dict:
    key_list = jax.random.split(jax.random.key(seed), 12)
    own_keys = jax.random.split(jax.random.fold_in(key_list[11], part), 12)
    return {
        "grid_state": centred(own_keys[0], (ENSEMBLE_SIZE, FIELD_COUNT, LEVELS, NLAT, NLON), 1.0, 6.0, ((0, 2), (2, 2), (3, 4))),
        "wave_slots": jax.random.permutation(key_list[1], M).astype(jnp.int32),
        "lat_basis": centred(key_list[2], (M, M, NLAT), NLAT ** -0.5, 0.25, ((0, 8),)),
        "vert_modes": draw_vert_modes(jax.random.fold_in(key_list[11], 71), part),
        "vert_rates": jnp.clip(jnp.exp(jax.random.uniform(key_list[4], (FIELD_COUNT, LEVELS), jnp.float32, math.log(0.05), math.log(20.0))), 0.05, 20.0),
        "band_sizes": ragged(key_list[5], BANDS, NLAT, BAND_MOST, 2).astype(jnp.int32),
        "norm_gain": jnp.clip(1.0 + 0.15 * jax.random.normal(key_list[6], (FEAT,), jnp.float32), 0.25, 1.75),
        "w_in": centred(key_list[7], (UNITS, FEAT), FEAT ** -0.5, 1.25),
        "band_bias": centred(key_list[8], (UNITS, BANDS), 1.0, 6.0, (), jnp.float32),
        "w_mid": centred(key_list[9], (UNITS, UNITS), UNITS ** -0.5, 0.25),
        "w_out": centred(key_list[10], (FEAT, UNITS), UNITS ** -0.5, 0.25),
    }


transport_speed = 0.5
norm_eps = 1e-06

def fourier_tables(wave_slots, lon_count):
    wave_count = wave_slots.shape[0]
    longitude = jnp.arange(lon_count, dtype=jnp.int32)
    integer_phase = longitude[:, None] * wave_slots[None, :] % lon_count
    phase_angle = integer_phase.astype(jnp.float32) * (2.0 * math.pi / lon_count)
    table_scale = 1.0 / math.sqrt(lon_count)
    cosine = jnp.cos(phase_angle) * table_scale
    sine_part = jnp.sin(phase_angle) * table_scale
    forward = jnp.stack([cosine, -sine_part], axis=1).reshape(lon_count, 2 * wave_count).astype(jnp.bfloat16)
    weight = jnp.where(wave_slots == 0, 1.0, 2.0).astype(jnp.float32)
    inverse = jnp.stack([cosine.T * weight[:, None], -sine_part.T * weight[:, None]], axis=0).astype(jnp.bfloat16)
    return (forward, inverse)

def advection_term(padded, main_band_entries):
    above_main_entries = padded[:, :, :, 2:, :].astype(jnp.float32)
    below_main_entries = padded[:, :, :, :-2, :].astype(jnp.float32)
    oscillation_factor = jnp.roll(main_band_entries, -1, axis=1).astype(jnp.float32)
    return (main_band_entries.astype(jnp.float32) + transport_speed * oscillation_factor * (above_main_entries - below_main_entries)).astype(jnp.bfloat16)

def couple(spectra, wave_part, vert_modes, vert_rates):
    wave_count = spectra.shape[-1]
    degree = wave_part[:, None] + jnp.arange(wave_count, dtype=jnp.int32)[None, :]
    spectra = jnp.where((degree < wave_count)[:, None, None, None, None, :], spectra, 0.0)
    curvature = (degree * (degree + 1)).astype(jnp.float32) / float(wave_count * wave_count)
    vorticity = spectra[:, :, 0] / (1.0 + curvature[:, None, None, None, :] * vert_rates[0][None, None, :, None, None])
    coupled_part = spectra[:, :, 1:]
    modal = jnp.einsum('sbflrk,li->sbfirk', coupled_part, vert_modes, precision=lax.Precision.HIGHEST)
    scaled = modal / (1.0 + curvature[:, None, None, None, None, :] * vert_rates[1:][None, None, :, :, None, None])
    restored = jnp.einsum('sbfirk,li->sbflrk', scaled, vert_modes, precision=lax.Precision.HIGHEST)
    return jnp.concatenate([vorticity[:, :, None], restored], axis=2)

def column_net(grid_cols, lat_first, band_sizes, norm_gain, w_in, band_bias, w_mid, w_out):
    members, fields, levels, lat_rows, lon_cells = grid_cols.shape
    unit_count = w_in.shape[0]
    values = grid_cols.reshape(members, fields * levels, lat_rows * lon_cells).astype(jnp.float32)
    average_squared = lax.optimization_barrier(jnp.mean(values * values, axis=1, keepdims=True))
    rescaled_values = (values * lax.rsqrt(average_squared + norm_eps) * norm_gain[None, :, None]).astype(jnp.bfloat16)
    rescaled_values = lax.optimization_barrier(rescaled_values)
    band_ends = jnp.cumsum(band_sizes).astype(jnp.int32)
    band_starts = band_ends - band_sizes
    latitude = lat_first + jnp.arange(lat_rows, dtype=jnp.int32)
    inside = ((latitude[None, :] >= band_starts[:, None]) & (latitude[None, :] < band_ends[:, None])).astype(jnp.float32)
    lat_bias = jnp.dot(band_bias, inside, precision=lax.Precision.HIGHEST)
    cell_bias = jnp.broadcast_to(lat_bias[:, :, None], (unit_count, lat_rows, lon_cells)).reshape(unit_count, lat_rows * lon_cells)
    first_layer = jnp.einsum('hf,bfc->bhc', w_in.astype(jnp.float32), rescaled_values.astype(jnp.float32))
    first_layer = lax.optimization_barrier(jax.nn.silu(first_layer + cell_bias[None]).astype(jnp.bfloat16))
    second = jnp.einsum('hg,bgc->bhc', w_mid.astype(jnp.float32), first_layer.astype(jnp.float32))
    second = lax.optimization_barrier(jax.nn.silu(second).astype(jnp.bfloat16))
    increment = jnp.einsum('fh,bhc->bfc', w_out.astype(jnp.float32), second.astype(jnp.float32))
    return (values + increment).astype(jnp.bfloat16).reshape(grid_cols.shape)

def reference(grid_state, wave_slots, lat_basis, vert_modes, vert_rates, band_sizes, norm_gain, w_in, band_bias, w_mid, w_out):
    members, fields, levels, lat_count, lon_count = grid_state.shape
    wave_count = wave_slots.shape[0]
    slot_block = 8
    lat_block = 8
    padded = jnp.pad(grid_state, ((0, 0), (0, 0), (0, 0), (1, 1), (0, 0)))
    advected = advection_term(padded, grid_state)
    forward, inverse = fourier_tables(wave_slots, lon_count)
    coeffs = jnp.dot(advected.reshape(-1, lon_count).astype(jnp.float32), forward.astype(jnp.float32), preferred_element_type=jnp.float32).astype(jnp.bfloat16)
    coeffs = coeffs.reshape(members, fields, levels, lat_count, 2, wave_count)
    by_slot = jnp.moveaxis(coeffs, 5, 0).reshape(wave_count // slot_block, slot_block, members, fields, levels, lat_count, 2)
    basis_blocks = lat_basis.reshape(wave_count // slot_block, slot_block, wave_count, lat_count)
    wave_blocks = wave_slots.reshape(wave_count // slot_block, slot_block)

    def legendre(operands):
        basis_part, coeff_part, wave_part = operands
        raw_spectra = jnp.einsum('skj,sbfljr->sbflrk', basis_part.astype(jnp.float32), coeff_part.astype(jnp.float32))
        coupled = couple(raw_spectra, wave_part, vert_modes, vert_rates)
        rounded = lax.optimization_barrier(coupled.astype(jnp.bfloat16))
        back_part = jnp.einsum('skj,sbflrk->sbflrj', basis_part.astype(jnp.float32), rounded.astype(jnp.float32))
        return (coupled, back_part.astype(jnp.bfloat16))
    coupled_blocks, back_blocks = lax.map(legendre, (basis_blocks, by_slot, wave_blocks))
    spectral = coupled_blocks.reshape(wave_count, members, fields, levels, 2, wave_count)
    back_fourier = back_blocks.reshape(wave_count, members, fields, levels, 2, lat_count)
    grid_mid = jnp.einsum('pbflrj,rpi->bflji', back_fourier.astype(jnp.float32), inverse.astype(jnp.float32)).astype(jnp.bfloat16)
    lat_blocks = grid_mid.reshape(members, fields, levels, lat_count // lat_block, lat_block, lon_count)
    lat_blocks = jnp.moveaxis(lat_blocks, 3, 0)
    starts = jnp.arange(lat_count // lat_block, dtype=jnp.int32) * lat_block

    def net_block(operands):
        lat_slab, slab_start = operands
        return column_net(lat_slab, slab_start, band_sizes, norm_gain, w_in, band_bias, w_mid, w_out)
    mixed_slabs = lax.map(net_block, (lat_blocks, starts))
    new_state = jnp.moveaxis(mixed_slabs, 0, 3).reshape(members, fields, levels, lat_count, lon_count)
    return (spectral, new_state)
```

```python
import functools
import math

import jax
import jax.numpy as jnp
from jax import lax
from jax.experimental import pallas as pl
from jax.experimental.pallas import tpu as pltpu
from jax.sharding import PartitionSpec as P

transport_speed = 0.5
norm_eps = 1e-06


def extended(array, sides, width):
    for axis, dim in sides:
        size, length = (lax.axis_size(axis), array.shape[dim])
        up = [(i, (i + 1) % size) for i in range(size - 1)]
        down = [(j, i) for i, j in up]
        last = lax.slice_in_dim(array, length - width, length, axis=dim)
        initial = lax.slice_in_dim(array, 0, width, axis=dim)
        before = lax.ppermute(last, axis, up)
        after = lax.ppermute(initial, axis, down)
        array = jnp.concatenate([before, array, after], axis=dim)
    return array


def fourier_tables(wave_slots, lon_count):
    wave_count = wave_slots.shape[0]
    longitude = jnp.arange(lon_count, dtype=jnp.int32)
    integer_phase = longitude[:, None] * wave_slots[None, :] % lon_count
    phase_angle = integer_phase.astype(jnp.float32) * (2.0 * math.pi / lon_count)
    table_scale = 1.0 / math.sqrt(lon_count)
    cosine = jnp.cos(phase_angle) * table_scale
    sine_part = jnp.sin(phase_angle) * table_scale
    forward = (
        jnp.stack([cosine, -sine_part], axis=1)
        .reshape(lon_count, 2 * wave_count)
        .astype(jnp.bfloat16)
    )
    weight = jnp.where(wave_slots == 0, 1.0, 2.0).astype(jnp.float32)
    inverse = jnp.stack(
        [cosine.T * weight[:, None], -sine_part.T * weight[:, None]], axis=0
    ).astype(jnp.bfloat16)
    return (forward, inverse)


def advection_term(padded, main_band_entries):
    above_main_entries = padded[:, :, :, 2:, :].astype(jnp.float32)
    below_main_entries = padded[:, :, :, :-2, :].astype(jnp.float32)
    oscillation_factor = jnp.roll(main_band_entries, -1, axis=1).astype(jnp.float32)
    return (
        main_band_entries.astype(jnp.float32)
        + transport_speed * oscillation_factor * (above_main_entries - below_main_entries)
    ).astype(jnp.bfloat16)


def couple(spectra, wave_part, vert_modes, vert_rates):
    wave_count = spectra.shape[-1]
    degree = wave_part[:, None] + jnp.arange(wave_count, dtype=jnp.int32)[None, :]
    spectra = jnp.where((degree < wave_count)[:, None, None, None, None, :], spectra, 0.0)
    curvature = (degree * (degree + 1)).astype(jnp.float32) / float(wave_count * wave_count)
    vorticity = spectra[:, :, 0] / (
        1.0 + curvature[:, None, None, None, :] * vert_rates[0][None, None, :, None, None]
    )
    coupled_part = spectra[:, :, 1:]
    modal = jnp.einsum(
        "sbflrk,li->sbfirk", coupled_part, vert_modes, precision=lax.Precision.HIGHEST
    )
    scaled = modal / (
        1.0 + curvature[:, None, None, None, None, :] * vert_rates[1:][None, None, :, :, None, None]
    )
    restored = jnp.einsum("sbfirk,li->sbflrk", scaled, vert_modes, precision=lax.Precision.HIGHEST)
    return jnp.concatenate([vorticity[:, :, None], restored], axis=2)


def column_net(grid_cols, lat_first, band_sizes, norm_gain, w_in, band_bias, w_mid, w_out):
    members, fields, levels, lat_rows, lon_cells = grid_cols.shape
    unit_count = w_in.shape[0]
    values = grid_cols.reshape(members, fields * levels, lat_rows * lon_cells).astype(jnp.float32)
    average_squared = jnp.mean(values * values, axis=1, keepdims=True)
    rescaled_values = (
        values * lax.rsqrt(average_squared + norm_eps) * norm_gain[None, :, None]
    ).astype(jnp.bfloat16)
    band_ends = jnp.cumsum(band_sizes)
    band_starts = band_ends - band_sizes
    latitude = lat_first + jnp.arange(lat_rows, dtype=jnp.int32)
    inside = (
        (latitude[None, :] >= band_starts[:, None]) & (latitude[None, :] < band_ends[:, None])
    ).astype(jnp.float32)
    lat_bias = jnp.dot(band_bias, inside, precision=lax.Precision.HIGHEST)
    cell_bias = jnp.broadcast_to(lat_bias[:, :, None], (unit_count, lat_rows, lon_cells)).reshape(
        unit_count, lat_rows * lon_cells
    )
    first_layer = jnp.einsum(
        "hf,bfc->bhc", w_in, rescaled_values, preferred_element_type=jnp.float32
    )
    first_layer = jax.nn.silu(first_layer + cell_bias[None]).astype(jnp.bfloat16)
    second = jnp.einsum("hg,bgc->bhc", w_mid, first_layer, preferred_element_type=jnp.float32)
    second = jax.nn.silu(second).astype(jnp.bfloat16)
    increment = jnp.einsum("fh,bhc->bfc", w_out, second, preferred_element_type=jnp.float32)
    return (values + increment).astype(jnp.bfloat16).reshape(grid_cols.shape)


def local_plain(
    grid_state,
    wave_slots,
    lat_basis,
    vert_modes,
    vert_rates,
    band_sizes,
    norm_gain,
    w_in,
    band_bias,
    w_mid,
    w_out,
):
    members, fields, lev_dev, lat_dev, lon_count = grid_state.shape
    wide_count = lax.axis_size("wide")
    lev_count = lax.axis_size("lev")
    slot_dev, wave_count, lat_count = lat_basis.shape
    levels = lev_dev * lev_count
    padded = extended(grid_state, (("wide", 3),), 1)
    advected = advection_term(padded, grid_state)
    forward, inverse = fourier_tables(wave_slots, lon_count)
    coeffs = jnp.dot(
        advected.reshape(-1, lon_count), forward, preferred_element_type=jnp.float32
    ).astype(jnp.bfloat16)
    coeffs = coeffs.reshape(members, fields, lev_dev, lat_dev, 2, wide_count, lev_count, slot_dev)
    by_wave = lax.all_to_all(
        lax.all_to_all(coeffs, "wide", split_axis=5, concat_axis=3, tiled=True),
        "lev",
        split_axis=6,
        concat_axis=2,
        tiled=True,
    )
    by_wave = by_wave.reshape(members, fields, levels, lat_count, 2, slot_dev)
    block_index = lax.axis_index("wide") * lev_count + lax.axis_index("lev")
    first_slot = block_index * slot_dev
    wave_part = lax.dynamic_slice_in_dim(wave_slots, first_slot, slot_dev)
    raw_spectra = jnp.einsum(
        "skj,bfljrs->sbflrk", lat_basis, by_wave, preferred_element_type=jnp.float32
    )
    spectral = couple(raw_spectra, wave_part, vert_modes, vert_rates)
    rounded = spectral.astype(jnp.bfloat16)
    back_coeffs = jnp.einsum(
        "skj,sbflrk->sbflrj", lat_basis, rounded, preferred_element_type=jnp.float32
    ).astype(jnp.bfloat16)
    lat_quarter = lat_count // (wide_count * lev_count)
    parcel = back_coeffs.reshape(
        1, 1, slot_dev, members, fields, levels, 2, wide_count, lev_count, lat_quarter
    )
    arrived = lax.all_to_all(
        lax.all_to_all(parcel, "wide", split_axis=7, concat_axis=0, tiled=True),
        "lev",
        split_axis=8,
        concat_axis=1,
        tiled=True,
    )
    arrived = arrived.reshape(wave_count, members, fields, levels, 2, lat_quarter)
    grid_mid = jnp.einsum(
        "pbflrj,rpi->bflji", arrived, inverse, preferred_element_type=jnp.float32
    ).astype(jnp.bfloat16)
    new_state = column_net(
        grid_mid, block_index * lat_quarter, band_sizes, norm_gain, w_in, band_bias, w_mid, w_out
    )
    return (spectral, new_state)


LANES = 128
PACK = 16
VMEM_BYTES = 58 * 2**20


def angle_parts(slot_waves, lon_count):
    coarse = jnp.arange(lon_count // LANES, dtype=jnp.int32) * LANES
    fine = jnp.arange(LANES, dtype=jnp.int32)

    def angles(longitude):
        phase = slot_waves[:, None] * longitude[None, :] % lon_count
        return phase.astype(jnp.float32) * (2.0 * math.pi / lon_count)

    a, b = angles(coarse), angles(fine)
    scale = 1.0 / math.sqrt(lon_count)
    return jnp.cos(a), jnp.sin(a), jnp.cos(b) * scale, jnp.sin(b) * scale


def table_kernel(devices, ca_ref, sa_ref, cb_ref, sb_ref, out_ref):
    slots, tiles = ca_ref.shape
    per = slots // devices
    cb, sb = cb_ref[...], sb_ref[...]
    for t in range(tiles):
        ca, sa = ca_ref[:, t : t + 1], sa_ref[:, t : t + 1]
        cosine = (ca * cb - sa * sb).astype(jnp.bfloat16)
        minus_sine = (-(sa * cb + ca * sb)).astype(jnp.bfloat16)
        cols = slice(t * LANES, (t + 1) * LANES)
        for d in range(devices):
            rows = slice(d * per, (d + 1) * per)
            out_ref[d, 0, :, cols] = cosine[rows]
            out_ref[d, 1, :, cols] = minus_sine[rows]


def fourier_kernel(x_ref, next_ref, before_ref, after_ref, table_ref, out_ref):
    _, levels, rows, _ = x_ref.shape
    parts = []
    row = lax.broadcasted_iota(jnp.int32, (rows, 1), 0)
    for l in range(levels):
        x = x_ref[0, l].astype(jnp.float32)
        up = jnp.where(row == rows - 1, after_ref[0, l].astype(jnp.float32), pltpu.roll(x, rows - 1, 0))
        down = jnp.where(row == 0, before_ref[0, l].astype(jnp.float32), pltpu.roll(x, 1, 0))
        mixed = x + transport_speed * next_ref[0, l].astype(jnp.float32) * (up - down)
        parts.append(mixed.astype(jnp.bfloat16))
    advected = jnp.concatenate(parts, axis=0)
    out_ref[...] = lax.dot_general(
        table_ref[...], advected, (((1,), (1,)), ((), ())), preferred_element_type=jnp.float32
    ).astype(jnp.bfloat16)


def fourier(grid_state, before, after, table):
    _, fields, lev_dev, lat_dev, lon_count = grid_state.shape
    x, before, after = grid_state[0], before[0], after[0]
    pair = 2 if lev_dev % 2 == 0 else 1
    rows = table.shape[0]
    halves = lev_dev // pair
    return pl.pallas_call(
        fourier_kernel,
        grid=(fields, halves),
        in_specs=[
            pl.BlockSpec((1, pair, lat_dev, lon_count), lambda f, h: (f, h, 0, 0)),
            pl.BlockSpec((1, pair, lat_dev, lon_count), lambda f, h: (lax.rem(f + 1, fields), h, 0, 0)),
            pl.BlockSpec((1, pair, 1, lon_count), lambda f, h: (f, h, 0, 0)),
            pl.BlockSpec((1, pair, 1, lon_count), lambda f, h: (f, h, 0, 0)),
            pl.BlockSpec((rows, lon_count), lambda f, h: (0, 0)),
        ],
        out_specs=pl.BlockSpec((rows, pair * lat_dev), lambda f, h: (0, f * halves + h)),
        out_shape=jax.ShapeDtypeStruct((rows, fields * lev_dev * lat_dev), jnp.bfloat16),
        compiler_params=pltpu.CompilerParams(vmem_limit_bytes=VMEM_BYTES),
        cost_estimate=pl.CostEstimate(
            flops=2 * rows * lon_count * fields * lev_dev * lat_dev,
            bytes_accessed=4 * rows * fields * lev_dev * lat_dev,
            transcendentals=0,
        ),
    )(x, x, before, after, table)


def legendre_kernel(
    dims, rates_ref, modes_ref, wave_ref, x_ref, basis_ref, spec_ref, *rest
):
    fields, levels, lev_dev, lev_count, subs, parts = dims
    y_refs, (flat_ref, work_ref) = rest[: len(parts)], rest[len(parts) :]
    group, wave_count, lat_count = basis_ref.shape
    cols = fields * 2 * levels
    tiles = lat_count // LANES
    wave_tiles = wave_count // LANES
    wide_count = x_ref.shape[0] // lev_count
    per_tile = lat_count // wide_count // LANES
    jw = LANES // levels

    def place(f, r, l):
        return (f * 2 + r) * levels + l

    for w in range(wide_count):
        for lx in range(lev_count):
            for f in range(fields):
                for l in range(lev_dev):
                    for p in range(per_tile):
                        lane = ((f * lev_dev + l) * per_tile + p) * LANES
                        for r in range(2):
                            block = x_ref[w * lev_count + lx, r, :, lane : lane + LANES].astype(jnp.float32)
                            start = place(f, r, lx * lev_dev + l)
                            for h in range(group // 8):
                                flat_ref[w * per_tile + p, pl.ds(start + h * 8 * cols, 8, stride=cols), :] = block[
                                    h * 8 : (h + 1) * 8
                                ]

    def forward(s, carry):
        rows = pl.ds(pl.multiple_of(s * cols, 8), cols)
        lhs = jnp.concatenate([flat_ref[t, rows, :].astype(jnp.bfloat16) for t in range(tiles)], axis=1)
        raw = lax.dot_general(
            lhs, basis_ref[s], (((1,), (1,)), ((), ())), preferred_element_type=jnp.float32
        )
        for t in range(wave_tiles):
            work_ref[t, rows, :] = raw[:, t * LANES : (t + 1) * LANES]
        return carry

    lax.fori_loop(0, group, forward, 0, unroll=4)

    def couple_tile(step, carry):
        t, h = lax.div(step, group // 8), lax.rem(step, group // 8)
        slot0 = pl.multiple_of(h * 8, 8)
        wave = wave_ref[pl.ds(slot0, 8), :]
        degree = wave + lax.broadcasted_iota(jnp.int32, (8, LANES), 1) + t * LANES
        inside = degree < wave_count
        curvature = (degree * (degree + 1)).astype(jnp.float32) * (1.0 / float(wave_count * wave_count))
        for f in range(fields):
            gains = [
                jnp.where(inside, 1.0 / (1.0 + curvature * rates_ref[f, l]), 0.0) for l in range(levels)
            ]
            for r in range(2):
                where = [pl.ds(slot0 * cols + place(f, r, l), 8, stride=cols) for l in range(levels)]
                raw = [work_ref[t, where[l], :] for l in range(levels)]
                if f == 0:
                    spectral = [raw[l] * gains[l] for l in range(levels)]
                else:
                    scaled = []
                    for i in range(levels):
                        total = raw[0] * modes_ref[0, i]
                        for l in range(1, levels):
                            total = total + raw[l] * modes_ref[l, i]
                        scaled.append(total * gains[i])
                    spectral = []
                    for l in range(levels):
                        total = scaled[0] * modes_ref[l, 0]
                        for i in range(1, levels):
                            total = total + scaled[i] * modes_ref[l, i]
                        spectral.append(total)
                for l in range(levels):
                    work_ref[t, where[l], :] = spectral[l]
                    per_slot = fields * levels * wave_tiles * 2
                    row = ((f * levels + l) * wave_tiles + t) * 2 + r
                    spec_ref[pl.ds(slot0 * per_slot + row, 8, stride=per_slot), :] = spectral[l]
        return carry

    lax.fori_loop(0, wave_tiles * (group // 8), couple_tile, 0)

    def backward(s, carry):
        rows = pl.ds(pl.multiple_of(s * cols, 8), cols)
        lhs = jnp.concatenate(
            [work_ref[t, rows, :].astype(jnp.bfloat16) for t in range(wave_tiles)], axis=1
        )
        back = jnp.dot(lhs, basis_ref[s], preferred_element_type=jnp.float32)
        for t in range(tiles):
            flat_ref[t, rows, :] = back[:, t * LANES : (t + 1) * LANES]
        return carry

    lax.fori_loop(0, group, backward, 0, unroll=4)

    lane = lax.broadcasted_iota(jnp.int32, (8, LANES), 1)
    weights = [
        jnp.where(wave_ref[h * 8 : (h + 1) * 8, :] == 0, 1.0, 2.0) for h in range(group // 8)
    ]
    part_of = {}
    for index, members in enumerate(parts):
        for place_in, sub in enumerate(members):
            part_of[sub] = (index, place_in)
    dest_per_tile = levels // subs if levels >= subs else 1

    def scatter(t, carry):
        for f in range(fields):
            for r in range(2):
                halves = []
                for h in range(group // 8):
                    start = h * 8 * cols
                    pieces = [
                        flat_ref[t, pl.ds(start + place(f, r, l), 8, stride=cols), :] * weights[h]
                        for l in range(levels)
                    ]
                    bit = 1
                    while bit < levels:
                        shift = bit * jw
                        odd = (lane // shift) % 2 == 1
                        swapped = list(pieces)
                        for l in range(levels):
                            if l & bit == 0:
                                low, high = pieces[l], pieces[l | bit]
                                swapped[l] = jnp.where(odd, pltpu.roll(high, shift, 1), low)
                                swapped[l | bit] = jnp.where(odd, high, pltpu.roll(low, LANES - shift, 1))
                        pieces = swapped
                        bit *= 2
                    halves.append(pieces)
                for g in range(levels):
                    block = jnp.concatenate([half[g] for half in halves], axis=0).astype(jnp.bfloat16)
                    index, place_in = part_of[g % subs]
                    y_refs[index][t * dest_per_tile + g // subs, place_in, f, r] = block
        return carry

    lax.fori_loop(0, tiles, scatter, 0)


def legendre(received, lat_basis, wave_part, vert_modes, vert_rates, dims):
    fields, levels, lev_dev, lev_count, subs, parts = dims
    devices = received.shape[0]
    slots, wave_count, lat_count = lat_basis.shape
    group = PACK
    lanes_in = received.shape[-1]
    cols = fields * 2 * levels
    per_slot = fields * levels * (wave_count // LANES) * 2
    outs = pl.pallas_call(
        functools.partial(legendre_kernel, dims),
        grid=(slots // group,),
        in_specs=[
            pl.BlockSpec(memory_space=pltpu.SMEM),
            pl.BlockSpec(memory_space=pltpu.SMEM),
            pl.BlockSpec((group, 1), lambda g: (g, 0)),
            pl.BlockSpec((devices, 2, group, lanes_in), lambda g: (0, 0, g, 0)),
            pl.BlockSpec((group, wave_count, lat_count), lambda g: (g, 0, 0)),
        ],
        out_specs=[pl.BlockSpec((group * per_slot, LANES), lambda g: (g, 0))]
        + [
            pl.BlockSpec((devices, len(p), fields, 2, group, LANES), lambda g: (0, 0, 0, 0, g, 0))
            for p in parts
        ],
        out_shape=[jax.ShapeDtypeStruct((slots * per_slot, LANES), jnp.float32)]
        + [
            jax.ShapeDtypeStruct((devices, len(p), fields, 2, slots, LANES), jnp.bfloat16) for p in parts
        ],
        scratch_shapes=[
            pltpu.VMEM((lat_count // LANES, group * cols, LANES), jnp.float32),
            pltpu.VMEM((wave_count // LANES, group * cols, LANES), jnp.float32),
        ],
        compiler_params=pltpu.CompilerParams(vmem_limit_bytes=VMEM_BYTES),
        cost_estimate=pl.CostEstimate(
            flops=4 * slots * cols * wave_count * lat_count,
            bytes_accessed=2 * slots * wave_count * lat_count,
            transcendentals=0,
        ),
    )(vert_rates, vert_modes, wave_part[:, None], received.reshape(devices, 2, slots, lanes_in), lat_basis)
    spec, parcels = outs[0], outs[1:]
    spec = spec.reshape(slots, fields, levels, wave_count // LANES, 2, LANES)
    spec = spec.transpose(0, 1, 2, 4, 3, 5).reshape(slots, 1, fields, levels, 2, wave_count)
    return spec, parcels


def column_kernel(
    shape, band_ref, y_ref, table_ref, w_in_ref, w_mid_ref, w_out_ref, gain_ref, *rest
):
    fields, levels, jw, padded = shape
    out_ref, grid_ref, done_ref = rest[-3:]
    features = fields * levels
    subs = y_ref.shape[1]
    lon_count = table_ref.shape[1]
    lon_tiles = lon_count // LANES
    depth = table_ref.shape[0]
    bands = (w_in_ref.shape[1] - padded) // 3
    row = lax.broadcasted_iota(jnp.int32, (3 * bands, lon_count), 0)
    for sub in range(subs):
        lhs = jnp.concatenate(
            [y_ref[:, sub, f].reshape(depth, LANES) for f in range(fields)], axis=1
        )
        grid_mid = lax.dot_general(
            lhs, table_ref[...], (((0,), (0,)), ((), ())), preferred_element_type=jnp.float32
        )
        grid_mid = grid_mid.astype(jnp.bfloat16).astype(jnp.float32)
        for t in range(lon_tiles):
            grid_ref[t] = grid_mid[:, t * LANES : (t + 1) * LANES]

        def one_row(j, carry):
            where = pl.ds(j, features, stride=jw)
            x = jnp.concatenate([grid_ref[t, where, :] for t in range(lon_tiles)], axis=1)
            mean = jnp.sum(x * x, axis=0, keepdims=True) * (1.0 / features)
            normed = x * lax.rsqrt(mean + norm_eps) * gain_ref[...]
            if padded > features:
                normed = jnp.concatenate(
                    [normed, jnp.zeros((padded - features, lon_count), jnp.float32)], axis=0
                )
            chosen = lax.rem(row, bands) == band_ref[sub * jw + j]
            entries = jnp.concatenate(
                [normed.astype(jnp.bfloat16), jnp.where(chosen, 1.0, 0.0).astype(jnp.bfloat16)], axis=0
            )
            half = jnp.dot(w_in_ref[...], entries, preferred_element_type=jnp.float32)
            hidden = (half * jnp.tanh(half) + half).astype(jnp.bfloat16)
            half = jnp.dot(w_mid_ref[...], hidden, preferred_element_type=jnp.float32)
            hidden = (half * jnp.tanh(half) + half).astype(jnp.bfloat16)
            grown = jnp.dot(w_out_ref[...], hidden, preferred_element_type=jnp.float32)
            result = x + grown[:features]
            for t in range(lon_tiles):
                done_ref[t, where, :] = result[:, t * LANES : (t + 1) * LANES]
            return carry

        lax.fori_loop(0, jw, one_row, 0)
        for t in range(lon_tiles):
            out_ref[:, sub * jw : (sub + 1) * jw, t * LANES : (t + 1) * LANES] = (
                done_ref[t].reshape(features, jw, LANES).astype(jnp.bfloat16)
            )


def column_part(arrived, table, bands_here, weights, so_far, first, lat_quarter, dims):
    fields, levels, jw = dims
    w_in, w_mid, w_out, gain, padded = weights
    subs = arrived.shape[1]
    features = fields * levels
    depth, lon_count = table.shape
    rows = subs * jw
    whole = pl.BlockSpec(memory_space=pltpu.VMEM)
    args = [bands_here, arrived, table, w_in, w_mid, w_out, gain]
    specs = [pl.BlockSpec(memory_space=pltpu.SMEM)] + [whole] * 6
    aliases = {}
    if so_far is not None:
        args.append(so_far)
        specs.append(pl.BlockSpec(memory_space=pl.ANY))
        aliases = {len(args) - 1: 0}
    block = first // rows
    units = w_mid.shape[0]
    return pl.pallas_call(
        functools.partial(column_kernel, (fields, levels, jw, padded)),
        grid=(1,),
        in_specs=specs,
        out_specs=pl.BlockSpec((features, rows, lon_count), lambda g: (0, block, 0)),
        out_shape=jax.ShapeDtypeStruct((features, lat_quarter, lon_count), jnp.bfloat16),
        input_output_aliases=aliases,
        scratch_shapes=[
            pltpu.VMEM((lon_count // LANES, features * jw, LANES), jnp.float32),
            pltpu.VMEM((lon_count // LANES, features * jw, LANES), jnp.float32),
        ],
        compiler_params=pltpu.CompilerParams(vmem_limit_bytes=VMEM_BYTES),
        cost_estimate=pl.CostEstimate(
            flops=2 * rows * lon_count * units * (units + 2 * 256) + 2 * depth * lon_count * features * rows,
            bytes_accessed=4 * features * rows * lon_count,
            transcendentals=2 * rows * lon_count * units,
        ),
    )(*args)


def local_tiled(
    grid_state, wave_slots, lat_basis, vert_modes, vert_rates, band_sizes, norm_gain, w_in, band_bias, w_mid, w_out
):
    _, fields, lev_dev, lat_dev, lon_count = grid_state.shape
    wide_count = lax.axis_size("wide")
    lev_count = lax.axis_size("lev")
    devices = wide_count * lev_count
    slot_dev, wave_count, lat_count = lat_basis.shape
    levels = lev_dev * lev_count
    lat_quarter = lat_count // devices
    jw = LANES // levels
    subs = lat_quarter // jw
    block_index = lax.axis_index("wide") * lev_count + lax.axis_index("lev")

    up = [(i, i + 1) for i in range(wide_count - 1)]
    down = [(j, i) for i, j in up]
    before = lax.ppermute(grid_state[:, :, :, lat_dev - 1 :], "wide", up)
    after = lax.ppermute(grid_state[:, :, :, :1], "wide", down)
    angle_arrays = angle_parts(wave_slots, lon_count)
    table = pl.pallas_call(
        functools.partial(table_kernel, devices),
        out_shape=jax.ShapeDtypeStruct((devices, 2, slot_dev, lon_count), jnp.bfloat16),
        compiler_params=pltpu.CompilerParams(vmem_limit_bytes=VMEM_BYTES),
    )(*angle_arrays).reshape(devices * 2 * slot_dev, lon_count)

    coeffs = fourier(grid_state, before, after, table)
    received = lax.all_to_all(
        coeffs.reshape(devices, 2 * slot_dev, coeffs.shape[1]),
        ("wide", "lev"),
        split_axis=0,
        concat_axis=0,
        tiled=True,
    )
    wave_part = lax.dynamic_slice_in_dim(wave_slots, block_index * slot_dev, slot_dev)
    count = 2 if subs % 2 == 0 else 1
    parts = tuple(
        tuple(range(i * subs // count, (i + 1) * subs // count)) for i in range(count)
    )
    dims = (fields, levels, lev_dev, lev_count, subs, parts)
    spectral, parcels = legendre(received, lat_basis, wave_part, vert_modes, vert_rates, dims)

    bands = band_sizes.shape[0]
    latitude = block_index * lat_quarter + jnp.arange(lat_quarter, dtype=jnp.int32)
    bands_here = jnp.sum(
        (latitude[:, None] >= jnp.cumsum(band_sizes)[None, :]).astype(jnp.int32), axis=1
    )
    features = fields * levels
    padded = -(-features // PACK) * PACK
    pieces, rest = [], band_bias
    for _ in range(3):
        piece = lax.reduce_precision(rest, 8, 7)
        pieces.append(piece.astype(jnp.bfloat16))
        rest = rest - piece
    half = jnp.bfloat16(0.5)
    w_first = jnp.concatenate(
        [jnp.pad(w_in, ((0, 0), (0, padded - features)))] + pieces, axis=1
    ) * half
    weights = (
        w_first,
        w_mid * half,
        jnp.pad(w_out, ((0, padded - features), (0, 0))),
        norm_gain[:, None],
        padded,
    )
    new_state = None
    for part, parcel in zip(parts, parcels):
        arrived = lax.all_to_all(parcel, ("wide", "lev"), split_axis=0, concat_axis=0, tiled=True)
        rows = slice(part[0] * jw, (part[-1] + 1) * jw)
        new_state = column_part(
            arrived, table, bands_here[rows], weights, new_state, part[0] * jw, lat_quarter, (fields, levels, jw)
        )
    return spectral, new_state.reshape(1, fields, levels, lat_quarter, lon_count)


def local(grid_state, wave_slots, lat_basis, *rest):
    members, _, lev_dev, lat_dev, lon_count = grid_state.shape
    lev_count = lax.axis_size("lev")
    slot_dev, wave_count, lat_count = lat_basis.shape
    levels = lev_dev * lev_count
    lat_quarter = lat_dev // lev_count
    fits = (
        members == 1
        and levels == 8
        and lat_dev % LANES == 0
        and lon_count % LANES == 0
        and wave_count % LANES == 0
        and slot_dev % PACK == 0
        and lat_quarter % (LANES // levels) == 0
        and lat_quarter <= LANES
    )
    chosen = local_tiled if fits else local_plain
    return chosen(grid_state, wave_slots, lat_basis, *rest)


def solution(mesh):
    placed = (
        P(("groups", "fld"), None, "lev", "wide", None),
        P(),
        P(("wide", "lev"), None, None),
        P(),
        P(),
        P(),
        P(),
        P(),
        P(),
        P(),
        P(),
    )
    return jax.shard_map(
        local,
        mesh=mesh,
        in_specs=placed,
        out_specs=(
            P(("wide", "lev"), ("groups", "fld"), None, None, None, None),
            P(("groups", "fld"), None, None, ("wide", "lev"), None),
        ),
        check_vma=False,
    )
```

```python
import functools
import math

import jax
import jax.numpy as jnp
from jax import lax
from jax.experimental import pallas as pl
from jax.experimental.pallas import tpu as pltpu
from jax.sharding import PartitionSpec as P

transport_speed = 0.5
norm_eps = 1e-06


def extended(array, sides, width):
    for axis, dim in sides:
        size, length = (lax.axis_size(axis), array.shape[dim])
        up = [(i, (i + 1) % size) for i in range(size - 1)]
        down = [(j, i) for i, j in up]
        last = lax.slice_in_dim(array, length - width, length, axis=dim)
        initial = lax.slice_in_dim(array, 0, width, axis=dim)
        before = lax.ppermute(last, axis, up)
        after = lax.ppermute(initial, axis, down)
        array = jnp.concatenate([before, array, after], axis=dim)
    return array


def fourier_tables(wave_slots, lon_count):
    wave_count = wave_slots.shape[0]
    longitude = jnp.arange(lon_count, dtype=jnp.int32)
    integer_phase = longitude[:, None] * wave_slots[None, :] % lon_count
    phase_angle = integer_phase.astype(jnp.float32) * (2.0 * math.pi / lon_count)
    table_scale = 1.0 / math.sqrt(lon_count)
    cosine = jnp.cos(phase_angle) * table_scale
    sine_part = jnp.sin(phase_angle) * table_scale
    forward = (
        jnp.stack([cosine, -sine_part], axis=1)
        .reshape(lon_count, 2 * wave_count)
        .astype(jnp.bfloat16)
    )
    weight = jnp.where(wave_slots == 0, 1.0, 2.0).astype(jnp.float32)
    inverse = jnp.stack(
        [cosine.T * weight[:, None], -sine_part.T * weight[:, None]], axis=0
    ).astype(jnp.bfloat16)
    return (forward, inverse)


def advection_term(padded, main_band_entries):
    above_main_entries = padded[:, :, :, 2:, :].astype(jnp.float32)
    below_main_entries = padded[:, :, :, :-2, :].astype(jnp.float32)
    oscillation_factor = jnp.roll(main_band_entries, -1, axis=1).astype(jnp.float32)
    return (
        main_band_entries.astype(jnp.float32)
        + transport_speed * oscillation_factor * (above_main_entries - below_main_entries)
    ).astype(jnp.bfloat16)


def couple(spectra, wave_part, vert_modes, vert_rates):
    wave_count = spectra.shape[-1]
    degree = wave_part[:, None] + jnp.arange(wave_count, dtype=jnp.int32)[None, :]
    spectra = jnp.where((degree < wave_count)[:, None, None, None, None, :], spectra, 0.0)
    curvature = (degree * (degree + 1)).astype(jnp.float32) / float(wave_count * wave_count)
    vorticity = spectra[:, :, 0] / (
        1.0 + curvature[:, None, None, None, :] * vert_rates[0][None, None, :, None, None]
    )
    coupled_part = spectra[:, :, 1:]
    modal = jnp.einsum(
        "sbflrk,li->sbfirk", coupled_part, vert_modes, precision=lax.Precision.HIGHEST
    )
    scaled = modal / (
        1.0 + curvature[:, None, None, None, None, :] * vert_rates[1:][None, None, :, :, None, None]
    )
    restored = jnp.einsum("sbfirk,li->sbflrk", scaled, vert_modes, precision=lax.Precision.HIGHEST)
    return jnp.concatenate([vorticity[:, :, None], restored], axis=2)


def column_net(grid_cols, lat_first, band_sizes, norm_gain, w_in, band_bias, w_mid, w_out):
    members, fields, levels, lat_rows, lon_cells = grid_cols.shape
    unit_count = w_in.shape[0]
    values = grid_cols.reshape(members, fields * levels, lat_rows * lon_cells).astype(jnp.float32)
    average_squared = jnp.mean(values * values, axis=1, keepdims=True)
    rescaled_values = (
        values * lax.rsqrt(average_squared + norm_eps) * norm_gain[None, :, None]
    ).astype(jnp.bfloat16)
    band_ends = jnp.cumsum(band_sizes)
    band_starts = band_ends - band_sizes
    latitude = lat_first + jnp.arange(lat_rows, dtype=jnp.int32)
    inside = (
        (latitude[None, :] >= band_starts[:, None]) & (latitude[None, :] < band_ends[:, None])
    ).astype(jnp.float32)
    lat_bias = jnp.dot(band_bias, inside, precision=lax.Precision.HIGHEST)
    cell_bias = jnp.broadcast_to(lat_bias[:, :, None], (unit_count, lat_rows, lon_cells)).reshape(
        unit_count, lat_rows * lon_cells
    )
    first_layer = jnp.einsum(
        "hf,bfc->bhc", w_in, rescaled_values, preferred_element_type=jnp.float32
    )
    first_layer = jax.nn.silu(first_layer + cell_bias[None]).astype(jnp.bfloat16)
    second = jnp.einsum("hg,bgc->bhc", w_mid, first_layer, preferred_element_type=jnp.float32)
    second = jax.nn.silu(second).astype(jnp.bfloat16)
    increment = jnp.einsum("fh,bhc->bfc", w_out, second, preferred_element_type=jnp.float32)
    return (values + increment).astype(jnp.bfloat16).reshape(grid_cols.shape)


def local_plain(
    grid_state,
    wave_slots,
    lat_basis,
    vert_modes,
    vert_rates,
    band_sizes,
    norm_gain,
    w_in,
    band_bias,
    w_mid,
    w_out,
):
    members, fields, lev_dev, lat_dev, lon_count = grid_state.shape
    wide_count = lax.axis_size("wide")
    lev_count = lax.axis_size("lev")
    slot_dev, wave_count, lat_count = lat_basis.shape
    levels = lev_dev * lev_count
    padded = extended(grid_state, (("wide", 3),), 1)
    advected = advection_term(padded, grid_state)
    forward, inverse = fourier_tables(wave_slots, lon_count)
    coeffs = jnp.dot(
        advected.reshape(-1, lon_count), forward, preferred_element_type=jnp.float32
    ).astype(jnp.bfloat16)
    coeffs = coeffs.reshape(members, fields, lev_dev, lat_dev, 2, wide_count, lev_count, slot_dev)
    by_wave = lax.all_to_all(
        lax.all_to_all(coeffs, "wide", split_axis=5, concat_axis=3, tiled=True),
        "lev",
        split_axis=6,
        concat_axis=2,
        tiled=True,
    )
    by_wave = by_wave.reshape(members, fields, levels, lat_count, 2, slot_dev)
    block_index = lax.axis_index("wide") * lev_count + lax.axis_index("lev")
    first_slot = block_index * slot_dev
    wave_part = lax.dynamic_slice_in_dim(wave_slots, first_slot, slot_dev)
    raw_spectra = jnp.einsum(
        "skj,bfljrs->sbflrk", lat_basis, by_wave, preferred_element_type=jnp.float32
    )
    spectral = couple(raw_spectra, wave_part, vert_modes, vert_rates)
    rounded = spectral.astype(jnp.bfloat16)
    back_coeffs = jnp.einsum(
        "skj,sbflrk->sbflrj", lat_basis, rounded, preferred_element_type=jnp.float32
    ).astype(jnp.bfloat16)
    lat_quarter = lat_count // (wide_count * lev_count)
    parcel = back_coeffs.reshape(
        1, 1, slot_dev, members, fields, levels, 2, wide_count, lev_count, lat_quarter
    )
    arrived = lax.all_to_all(
        lax.all_to_all(parcel, "wide", split_axis=7, concat_axis=0, tiled=True),
        "lev",
        split_axis=8,
        concat_axis=1,
        tiled=True,
    )
    arrived = arrived.reshape(wave_count, members, fields, levels, 2, lat_quarter)
    grid_mid = jnp.einsum(
        "pbflrj,rpi->bflji", arrived, inverse, preferred_element_type=jnp.float32
    ).astype(jnp.bfloat16)
    new_state = column_net(
        grid_mid, block_index * lat_quarter, band_sizes, norm_gain, w_in, band_bias, w_mid, w_out
    )
    return (spectral, new_state)


LANES = 128
PACK = 16
VMEM_BYTES = 58 * 2**20


def angle_parts(slot_waves, lon_count):
    coarse = jnp.arange(lon_count // LANES, dtype=jnp.int32) * LANES
    fine = jnp.arange(LANES, dtype=jnp.int32)

    def angles(longitude):
        phase = slot_waves[:, None] * longitude[None, :] % lon_count
        return phase.astype(jnp.float32) * (2.0 * math.pi / lon_count)

    a, b = angles(coarse), angles(fine)
    scale = 1.0 / math.sqrt(lon_count)
    return jnp.cos(a), jnp.sin(a), jnp.cos(b) * scale, jnp.sin(b) * scale


def table_kernel(ca_ref, sa_ref, cb_ref, sb_ref, out_ref):
    tiles = ca_ref.shape[1]
    chunks, devices, _, per, _ = out_ref.shape
    cb, sb = cb_ref[...], sb_ref[...]
    for t in range(tiles):
        ca, sa = ca_ref[:, t : t + 1], sa_ref[:, t : t + 1]
        cosine = (ca * cb - sa * sb).astype(jnp.bfloat16)
        minus_sine = (-(sa * cb + ca * sb)).astype(jnp.bfloat16)
        cols = slice(t * LANES, (t + 1) * LANES)
        for d in range(devices):
            for c in range(chunks):
                first = (d * chunks + c) * per
                out_ref[c, d, 0, :, cols] = cosine[first : first + per]
                out_ref[c, d, 1, :, cols] = minus_sine[first : first + per]


def fourier_kernel(x_ref, next_ref, before_ref, after_ref, table_ref, *out_refs):
    _, levels, rows, _ = x_ref.shape
    parts = []
    row = lax.broadcasted_iota(jnp.int32, (rows, 1), 0)
    for l in range(levels):
        x = x_ref[0, l].astype(jnp.float32)
        up = jnp.where(row == rows - 1, after_ref[0, l].astype(jnp.float32), pltpu.roll(x, rows - 1, 0))
        down = jnp.where(row == 0, before_ref[0, l].astype(jnp.float32), pltpu.roll(x, 1, 0))
        mixed = x + transport_speed * next_ref[0, l].astype(jnp.float32) * (up - down)
        parts.append(mixed.astype(jnp.bfloat16))
    advected = jnp.concatenate(parts, axis=0)
    coeffs = lax.dot_general(
        table_ref[...], advected, (((1,), (1,)), ((), ())), preferred_element_type=jnp.float32
    ).astype(jnp.bfloat16)
    rows = coeffs.shape[0] // len(out_refs)
    for c, out_ref in enumerate(out_refs):
        out_ref[...] = coeffs[c * rows : (c + 1) * rows]


def fourier(grid_state, before, after, table, chunks):
    _, fields, lev_dev, lat_dev, lon_count = grid_state.shape
    x, before, after = grid_state[0], before[0], after[0]
    pair = 2 if lev_dev % 2 == 0 else 1
    rows = table.shape[0]
    halves = lev_dev // pair
    return pl.pallas_call(
        fourier_kernel,
        grid=(fields, halves),
        in_specs=[
            pl.BlockSpec((1, pair, lat_dev, lon_count), lambda f, h: (f, h, 0, 0)),
            pl.BlockSpec((1, pair, lat_dev, lon_count), lambda f, h: (lax.rem(f + 1, fields), h, 0, 0)),
            pl.BlockSpec((1, pair, 1, lon_count), lambda f, h: (f, h, 0, 0)),
            pl.BlockSpec((1, pair, 1, lon_count), lambda f, h: (f, h, 0, 0)),
            pl.BlockSpec((rows, lon_count), lambda f, h: (0, 0)),
        ],
        out_specs=[pl.BlockSpec((rows // chunks, pair * lat_dev), lambda f, h: (0, f * halves + h))] * chunks,
        out_shape=[jax.ShapeDtypeStruct((rows // chunks, fields * lev_dev * lat_dev), jnp.bfloat16)] * chunks,
        compiler_params=pltpu.CompilerParams(vmem_limit_bytes=VMEM_BYTES),
        cost_estimate=pl.CostEstimate(
            flops=2 * rows * lon_count * fields * lev_dev * lat_dev,
            bytes_accessed=4 * rows * fields * lev_dev * lat_dev,
            transcendentals=0,
        ),
    )(x, x, before, after, table)


def legendre_kernel(
    dims, rates_ref, modes_ref, wave_ref, x_ref, basis_ref, *rest
):
    fields, levels, lev_dev, lev_count, subs, parts = dims
    rest = rest[-len(parts) - 3 :]
    spec_ref, y_refs, (flat_ref, work_ref) = rest[0], rest[1:-2], rest[-2:]
    group, wave_count, lat_count = basis_ref.shape
    cols = fields * 2 * levels
    tiles = lat_count // LANES
    wave_tiles = wave_count // LANES
    wide_count = x_ref.shape[0] // lev_count
    per_tile = lat_count // wide_count // LANES
    jw = LANES // levels

    def place(f, r, l):
        return (f * 2 + r) * levels + l

    for w in range(wide_count):
        for lx in range(lev_count):
            for f in range(fields):
                for l in range(lev_dev):
                    for p in range(per_tile):
                        lane = ((f * lev_dev + l) * per_tile + p) * LANES
                        for r in range(2):
                            block = x_ref[w * lev_count + lx, r, :, lane : lane + LANES].astype(jnp.float32)
                            start = place(f, r, lx * lev_dev + l)
                            for h in range(group // 8):
                                flat_ref[w * per_tile + p, pl.ds(start + h * 8 * cols, 8, stride=cols), :] = block[
                                    h * 8 : (h + 1) * 8
                                ]

    def forward(s, carry):
        rows = pl.ds(pl.multiple_of(s * cols, 8), cols)
        lhs = jnp.concatenate([flat_ref[t, rows, :].astype(jnp.bfloat16) for t in range(tiles)], axis=1)
        raw = lax.dot_general(
            lhs, basis_ref[s], (((1,), (1,)), ((), ())), preferred_element_type=jnp.float32
        )
        for t in range(wave_tiles):
            work_ref[t, rows, :] = raw[:, t * LANES : (t + 1) * LANES]
        return carry

    lax.fori_loop(0, group, forward, 0, unroll=16)

    def couple_tile(step, carry):
        t, h = lax.div(step, group // 8), lax.rem(step, group // 8)
        slot0 = pl.multiple_of(h * 8, 8)
        wave = wave_ref[pl.ds(slot0, 8), :]
        degree = wave + lax.broadcasted_iota(jnp.int32, (8, LANES), 1) + t * LANES
        inside = degree < wave_count
        curvature = (degree * (degree + 1)).astype(jnp.float32) * (1.0 / float(wave_count * wave_count))
        per_slot = fields * levels * wave_tiles * 2

        def gain(f, l):
            return jnp.where(inside, 1.0 / (1.0 + curvature * rates_ref[f, l]), 0.0)

        def where(f, r, l):
            return pl.ds(slot0 * cols + place(f, r, l), 8, stride=cols)

        def keep(f, r, l, value):
            work_ref[t, where(f, r, l), :] = value
            row = ((f * levels + l) * wave_tiles + t) * 2 + r
            spec_ref[pl.ds(slot0 * per_slot + row, 8, stride=per_slot), :] = value

        for l in range(levels):
            scale = gain(0, l)
            for r in range(2):
                keep(0, r, l, work_ref[t, where(0, r, l), :] * scale)
        for f in range(1, fields):
            raw = [[work_ref[t, where(f, r, l), :] for l in range(levels)] for r in range(2)]
            scaled = [[], []]
            for i in range(levels):
                totals = [raw[r][0] * modes_ref[0, i] for r in range(2)]
                for l in range(1, levels):
                    mode = modes_ref[l, i]
                    totals = [totals[r] + raw[r][l] * mode for r in range(2)]
                scale = gain(f, i)
                for r in range(2):
                    scaled[r].append(totals[r] * scale)
            for l in range(levels):
                totals = [scaled[r][0] * modes_ref[l, 0] for r in range(2)]
                for i in range(1, levels):
                    mode = modes_ref[l, i]
                    totals = [totals[r] + scaled[r][i] * mode for r in range(2)]
                for r in range(2):
                    keep(f, r, l, totals[r])
        return carry

    lax.fori_loop(0, wave_tiles * (group // 8), couple_tile, 0)

    def backward(s, carry):
        rows = pl.ds(pl.multiple_of(s * cols, 8), cols)
        lhs = jnp.concatenate(
            [work_ref[t, rows, :].astype(jnp.bfloat16) for t in range(wave_tiles)], axis=1
        )
        back = jnp.dot(lhs, basis_ref[s], preferred_element_type=jnp.float32)
        for t in range(tiles):
            flat_ref[t, rows, :] = back[:, t * LANES : (t + 1) * LANES]
        return carry

    lax.fori_loop(0, group, backward, 0, unroll=16)

    lane = lax.broadcasted_iota(jnp.int32, (8, LANES), 1)
    weights = [
        jnp.where(wave_ref[h * 8 : (h + 1) * 8, :] == 0, 1.0, 2.0) for h in range(group // 8)
    ]
    part_of = {}
    for index, members in enumerate(parts):
        for place_in, sub in enumerate(members):
            part_of[sub] = (index, place_in)
    dest_per_tile = levels // subs if levels >= subs else 1

    def scatter(t, carry):
        for f in range(fields):
            for r in range(2):
                halves = []
                for h in range(group // 8):
                    start = h * 8 * cols
                    pieces = [
                        flat_ref[t, pl.ds(start + place(f, r, l), 8, stride=cols), :] * weights[h]
                        for l in range(levels)
                    ]
                    bit = 1
                    while bit < levels:
                        shift = bit * jw
                        odd = (lane // shift) % 2 == 1
                        swapped = list(pieces)
                        for l in range(levels):
                            if l & bit == 0:
                                low, high = pieces[l], pieces[l | bit]
                                swapped[l] = jnp.where(odd, pltpu.roll(high, shift, 1), low)
                                swapped[l | bit] = jnp.where(odd, high, pltpu.roll(low, LANES - shift, 1))
                        pieces = swapped
                        bit *= 2
                    halves.append(pieces)
                for g in range(levels):
                    block = jnp.concatenate([half[g] for half in halves], axis=0).astype(jnp.bfloat16)
                    index, place_in = part_of[g % subs]
                    y_refs[index][t * dest_per_tile + g // subs, 0, place_in, f, r] = block
        return carry

    lax.fori_loop(0, tiles, scatter, 0)


def legendre(received, lat_basis, wave_part, vert_modes, vert_rates, chunk, so_far, dims):
    fields, levels, lev_dev, lev_count, subs, parts, chunks = dims
    devices = received.shape[0]
    slots, wave_count, lat_count = lat_basis.shape
    group = PACK
    lanes_in = received.shape[-1]
    here = slots // chunks
    steps = here // group
    cols = fields * 2 * levels
    per_slot = fields * levels * (wave_count // LANES) * 2
    args = [vert_rates, vert_modes, wave_part[:, None], received.reshape(devices, 2, here, lanes_in), lat_basis]
    aliases = {}
    if so_far is not None:
        kept = [0] + list(range(2, 1 + len(parts)))
        aliases = {len(args) + n: k for n, k in enumerate(kept)}
        args = args + [so_far[k] for k in kept]
    first = chunk * steps

    def part_spec(index, part):
        block = (devices, 1, len(part), fields, 2, group, LANES)
        if index == 0:
            return pl.BlockSpec(block, lambda g: (0, 0, 0, 0, 0, g, 0))
        return pl.BlockSpec(block, lambda g: (0, chunk, 0, 0, 0, g, 0))

    return pl.pallas_call(
        functools.partial(legendre_kernel, (fields, levels, lev_dev, lev_count, subs, parts)),
        grid=(steps,),
        in_specs=[
            pl.BlockSpec(memory_space=pltpu.SMEM),
            pl.BlockSpec(memory_space=pltpu.SMEM),
            pl.BlockSpec((group, 1), lambda g: (first + g, 0)),
            pl.BlockSpec((devices, 2, group, lanes_in), lambda g: (0, 0, g, 0)),
            pl.BlockSpec((group, wave_count, lat_count), lambda g: (first + g, 0, 0)),
        ]
        + [pl.BlockSpec(memory_space=pl.ANY)] * len(aliases),
        out_specs=[pl.BlockSpec((group * per_slot, LANES), lambda g: (first + g, 0))]
        + [part_spec(i, p) for i, p in enumerate(parts)],
        out_shape=[jax.ShapeDtypeStruct((slots * per_slot, LANES), jnp.float32)]
        + [
            jax.ShapeDtypeStruct(
                (devices, chunks if i else 1, len(p), fields, 2, here, LANES), jnp.bfloat16
            )
            for i, p in enumerate(parts)
        ],
        input_output_aliases=aliases,
        scratch_shapes=[
            pltpu.VMEM((lat_count // LANES, group * cols, LANES), jnp.float32),
            pltpu.VMEM((wave_count // LANES, group * cols, LANES), jnp.float32),
        ],
        compiler_params=pltpu.CompilerParams(vmem_limit_bytes=VMEM_BYTES),
        cost_estimate=pl.CostEstimate(
            flops=40 * here * cols * wave_count * lat_count,
            bytes_accessed=2 * here * wave_count * lat_count,
            transcendentals=0,
        ),
    )(*args)


def column_kernel(
    shape, band_ref, table_ref, w_in_ref, w_mid_ref, w_out_ref, gain_ref, *rest
):
    fields, levels, jw, padded, count = shape
    y_refs, (out_ref, grid_ref, done_ref) = rest[:count], rest[-3:]
    features = fields * levels
    subs = y_refs[0].shape[2]
    lon_count = table_ref.shape[1]
    lon_tiles = lon_count // LANES
    bands = (w_in_ref.shape[1] - padded) // 3
    row = lax.broadcasted_iota(jnp.int32, (3 * bands, lon_count), 0)
    for sub in range(subs):
        lhs = jnp.concatenate(
            [
                jnp.concatenate(
                    [
                        y_ref[:, c, sub, f].reshape(-1, LANES)
                        for y_ref in y_refs
                        for c in range(y_ref.shape[1])
                    ],
                    axis=0,
                )
                for f in range(fields)
            ],
            axis=1,
        )
        grid_mid = lax.dot_general(
            lhs, table_ref[...], (((0,), (0,)), ((), ())), preferred_element_type=jnp.float32
        )
        grid_mid = grid_mid.astype(jnp.bfloat16).astype(jnp.float32)
        for t in range(lon_tiles):
            grid_ref[t] = grid_mid[:, t * LANES : (t + 1) * LANES]

        def one_row(j, carry):
            where = pl.ds(j, features, stride=jw)
            x = jnp.concatenate([grid_ref[t, where, :] for t in range(lon_tiles)], axis=1)
            mean = jnp.sum(x * x, axis=0, keepdims=True) * (1.0 / features)
            normed = x * lax.rsqrt(mean + norm_eps) * gain_ref[...]
            if padded > features:
                normed = jnp.concatenate(
                    [normed, jnp.zeros((padded - features, lon_count), jnp.float32)], axis=0
                )
            chosen = lax.rem(row, bands) == band_ref[sub * jw + j]
            entries = jnp.concatenate(
                [normed.astype(jnp.bfloat16), jnp.where(chosen, 1.0, 0.0).astype(jnp.bfloat16)], axis=0
            )
            half = jnp.dot(w_in_ref[...], entries, preferred_element_type=jnp.float32)
            hidden = (half * jnp.tanh(half) + half).astype(jnp.bfloat16)
            half = jnp.dot(w_mid_ref[...], hidden, preferred_element_type=jnp.float32)
            hidden = (half * jnp.tanh(half) + half).astype(jnp.bfloat16)
            grown = jnp.dot(w_out_ref[...], hidden, preferred_element_type=jnp.float32)
            result = x + grown[:features]
            for t in range(lon_tiles):
                done_ref[t, where, :] = result[:, t * LANES : (t + 1) * LANES]
            return carry

        lax.fori_loop(0, jw, one_row, 0)
        for t in range(lon_tiles):
            out_ref[:, sub * jw : (sub + 1) * jw, t * LANES : (t + 1) * LANES] = (
                done_ref[t].reshape(features, jw, LANES).astype(jnp.bfloat16)
            )


def column_part(arrived, table, bands_here, weights, so_far, first, lat_quarter, dims):
    fields, levels, jw = dims
    w_in, w_mid, w_out, gain = weights
    padded = w_out.shape[0]
    subs = arrived[0].shape[2]
    features = fields * levels
    depth, lon_count = table.shape
    rows = subs * jw
    whole = pl.BlockSpec(memory_space=pltpu.VMEM)
    args = [bands_here, table, w_in, w_mid, w_out, gain] + list(arrived)
    specs = [pl.BlockSpec(memory_space=pltpu.SMEM)] + [whole] * (5 + len(arrived))
    aliases = {}
    if so_far is not None:
        args.append(so_far)
        specs.append(pl.BlockSpec(memory_space=pl.ANY))
        aliases = {len(args) - 1: 0}
    block = first // rows
    units = w_mid.shape[0]
    return pl.pallas_call(
        functools.partial(column_kernel, (fields, levels, jw, padded, len(arrived))),
        grid=(1,),
        in_specs=specs,
        out_specs=pl.BlockSpec((features, rows, lon_count), lambda g: (0, block, 0)),
        out_shape=jax.ShapeDtypeStruct((features, lat_quarter, lon_count), jnp.bfloat16),
        input_output_aliases=aliases,
        scratch_shapes=[
            pltpu.VMEM((lon_count // LANES, features * jw, LANES), jnp.float32),
            pltpu.VMEM((lon_count // LANES, features * jw, LANES), jnp.float32),
        ],
        compiler_params=pltpu.CompilerParams(vmem_limit_bytes=VMEM_BYTES),
        cost_estimate=pl.CostEstimate(
            flops=2 * rows * lon_count * units * (units + 2 * 256) + 2 * depth * lon_count * features * rows,
            bytes_accessed=4 * features * rows * lon_count,
            transcendentals=2 * rows * lon_count * units,
        ),
    )(*args)


def local_tiled(
    grid_state, wave_slots, lat_basis, vert_modes, vert_rates, band_sizes, norm_gain, w_in, band_bias, w_mid, w_out
):
    _, fields, lev_dev, lat_dev, lon_count = grid_state.shape
    wide_count = lax.axis_size("wide")
    lev_count = lax.axis_size("lev")
    devices = wide_count * lev_count
    slot_dev, wave_count, lat_count = lat_basis.shape
    levels = lev_dev * lev_count
    lat_quarter = lat_count // devices
    jw = LANES // levels
    subs = lat_quarter // jw
    block_index = lax.axis_index("wide") * lev_count + lax.axis_index("lev")

    chunks = 2 if slot_dev % (2 * PACK) == 0 else 1
    angle_arrays = angle_parts(wave_slots, lon_count)
    edges = (grid_state[:, :, :, lat_dev - 1 :], grid_state[:, :, :, :1])
    edges, angle_arrays = lax.optimization_barrier((edges, angle_arrays))
    up = [(i, i + 1) for i in range(wide_count - 1)]
    down = [(j, i) for i, j in up]
    before = lax.ppermute(edges[0], "wide", up)
    after = lax.ppermute(edges[1], "wide", down)
    table = pl.pallas_call(
        table_kernel,
        out_shape=jax.ShapeDtypeStruct(
            (chunks, devices, 2, slot_dev // chunks, lon_count), jnp.bfloat16
        ),
        compiler_params=pltpu.CompilerParams(vmem_limit_bytes=VMEM_BYTES),
    )(*angle_arrays).reshape(devices * 2 * slot_dev, lon_count)

    def exchange(parcel):
        return lax.all_to_all(parcel, ("wide", "lev"), split_axis=0, concat_axis=0, tiled=True)

    coeffs = fourier(grid_state, before, after, table, chunks)
    received = [exchange(c.reshape(devices, -1, c.shape[1])) for c in coeffs]
    wave_part = lax.dynamic_slice_in_dim(wave_slots, block_index * slot_dev, slot_dev)
    count = 2 if subs % 2 == 0 else 1
    parts = tuple(
        tuple(range(i * subs // count, (i + 1) * subs // count)) for i in range(count)
    )
    dims = (fields, levels, lev_dev, lev_count, subs, parts, chunks)
    bands = band_sizes.shape[0]
    latitude = block_index * lat_quarter + jnp.arange(lat_quarter, dtype=jnp.int32)
    bands_here = jnp.sum(
        (latitude[:, None] >= jnp.cumsum(band_sizes)[None, :]).astype(jnp.int32), axis=1
    )
    features = fields * levels
    padded = -(-features // PACK) * PACK
    pieces, rest = [], band_bias
    for _ in range(3):
        piece = lax.reduce_precision(rest, 8, 7)
        pieces.append(piece.astype(jnp.bfloat16))
        rest = rest - piece
    half = jnp.bfloat16(0.5)
    w_first = jnp.concatenate(
        [jnp.pad(w_in, ((0, 0), (0, padded - features)))] + pieces, axis=1
    ) * half
    weights = (
        w_first,
        w_mid * half,
        jnp.pad(w_out, ((0, padded - features), (0, 0))),
        norm_gain[:, None],
    )
    received[0], weights, bands_here = lax.optimization_barrier((received[0], weights, bands_here))
    so_far, arrived_first = None, []
    for c in range(chunks):
        so_far = legendre(received[c], lat_basis, wave_part, vert_modes, vert_rates, c, so_far, dims)
        parcel = so_far[1]
        if arrived_first:
            arrived_first[-1], parcel = lax.optimization_barrier((arrived_first[-1], parcel))
        arrived_first.append(exchange(parcel))
    spectral = so_far[0].reshape(slot_dev, fields, levels, wave_count // LANES, 2, LANES)
    spectral = spectral.transpose(0, 1, 2, 4, 3, 5).reshape(slot_dev, 1, fields, levels, 2, wave_count)

    new_state = None
    for index, part in enumerate(parts):
        arrived = [exchange(so_far[1 + index])] if index else arrived_first
        rows = slice(part[0] * jw, (part[-1] + 1) * jw)
        new_state = column_part(
            arrived, table, bands_here[rows], weights, new_state, part[0] * jw, lat_quarter, (fields, levels, jw)
        )
    return spectral, new_state.reshape(1, fields, levels, lat_quarter, lon_count)


def local(grid_state, wave_slots, lat_basis, *rest):
    members, _, lev_dev, lat_dev, lon_count = grid_state.shape
    lev_count = lax.axis_size("lev")
    slot_dev, wave_count, lat_count = lat_basis.shape
    levels = lev_dev * lev_count
    lat_quarter = lat_dev // lev_count
    fits = (
        members == 1
        and levels == 8
        and lat_dev % LANES == 0
        and lon_count % LANES == 0
        and wave_count % LANES == 0
        and slot_dev % PACK == 0
        and lat_quarter % (LANES // levels) == 0
        and lat_quarter <= LANES
    )
    chosen = local_tiled if fits else local_plain
    return chosen(grid_state, wave_slots, lat_basis, *rest)


def solution(mesh):
    placed = (
        P(("groups", "fld"), None, "lev", "wide", None),
        P(),
        P(("wide", "lev"), None, None),
        P(),
        P(),
        P(),
        P(),
        P(),
        P(),
        P(),
        P(),
    )
    return jax.shard_map(
        local,
        mesh=mesh,
        in_specs=placed,
        out_specs=(
            P(("wide", "lev"), ("groups", "fld"), None, None, None, None),
            P(("groups", "fld"), None, None, ("wide", "lev"), None),
        ),
        check_vma=False,
    )
```

```python
import functools
import math

import jax
import jax.numpy as jnp
from jax import lax
from jax.experimental import pallas as pl
from jax.experimental.pallas import tpu as pltpu
from jax.sharding import PartitionSpec as P

transport_speed = 0.5
norm_eps = 1e-06


def extended(array, sides, width):
    for axis, dim in sides:
        size, length = (lax.axis_size(axis), array.shape[dim])
        up = [(i, (i + 1) % size) for i in range(size - 1)]
        down = [(j, i) for i, j in up]
        last = lax.slice_in_dim(array, length - width, length, axis=dim)
        initial = lax.slice_in_dim(array, 0, width, axis=dim)
        before = lax.ppermute(last, axis, up)
        after = lax.ppermute(initial, axis, down)
        array = jnp.concatenate([before, array, after], axis=dim)
    return array


def fourier_tables(wave_slots, lon_count):
    wave_count = wave_slots.shape[0]
    longitude = jnp.arange(lon_count, dtype=jnp.int32)
    integer_phase = longitude[:, None] * wave_slots[None, :] % lon_count
    phase_angle = integer_phase.astype(jnp.float32) * (2.0 * math.pi / lon_count)
    table_scale = 1.0 / math.sqrt(lon_count)
    cosine = jnp.cos(phase_angle) * table_scale
    sine_part = jnp.sin(phase_angle) * table_scale
    forward = (
        jnp.stack([cosine, -sine_part], axis=1)
        .reshape(lon_count, 2 * wave_count)
        .astype(jnp.bfloat16)
    )
    weight = jnp.where(wave_slots == 0, 1.0, 2.0).astype(jnp.float32)
    inverse = jnp.stack(
        [cosine.T * weight[:, None], -sine_part.T * weight[:, None]], axis=0
    ).astype(jnp.bfloat16)
    return (forward, inverse)


def advection_term(padded, main_band_entries):
    above_main_entries = padded[:, :, :, 2:, :].astype(jnp.float32)
    below_main_entries = padded[:, :, :, :-2, :].astype(jnp.float32)
    oscillation_factor = jnp.roll(main_band_entries, -1, axis=1).astype(jnp.float32)
    return (
        main_band_entries.astype(jnp.float32)
        + transport_speed * oscillation_factor * (above_main_entries - below_main_entries)
    ).astype(jnp.bfloat16)


def couple(spectra, wave_part, vert_modes, vert_rates):
    wave_count = spectra.shape[-1]
    degree = wave_part[:, None] + jnp.arange(wave_count, dtype=jnp.int32)[None, :]
    spectra = jnp.where((degree < wave_count)[:, None, None, None, None, :], spectra, 0.0)
    curvature = (degree * (degree + 1)).astype(jnp.float32) / float(wave_count * wave_count)
    vorticity = spectra[:, :, 0] / (
        1.0 + curvature[:, None, None, None, :] * vert_rates[0][None, None, :, None, None]
    )
    coupled_part = spectra[:, :, 1:]
    modal = jnp.einsum(
        "sbflrk,li->sbfirk", coupled_part, vert_modes, precision=lax.Precision.HIGHEST
    )
    scaled = modal / (
        1.0 + curvature[:, None, None, None, None, :] * vert_rates[1:][None, None, :, :, None, None]
    )
    restored = jnp.einsum("sbfirk,li->sbflrk", scaled, vert_modes, precision=lax.Precision.HIGHEST)
    return jnp.concatenate([vorticity[:, :, None], restored], axis=2)


def column_net(grid_cols, lat_first, band_sizes, norm_gain, w_in, band_bias, w_mid, w_out):
    members, fields, levels, lat_rows, lon_cells = grid_cols.shape
    unit_count = w_in.shape[0]
    values = grid_cols.reshape(members, fields * levels, lat_rows * lon_cells).astype(jnp.float32)
    average_squared = jnp.mean(values * values, axis=1, keepdims=True)
    rescaled_values = (
        values * lax.rsqrt(average_squared + norm_eps) * norm_gain[None, :, None]
    ).astype(jnp.bfloat16)
    band_ends = jnp.cumsum(band_sizes)
    band_starts = band_ends - band_sizes
    latitude = lat_first + jnp.arange(lat_rows, dtype=jnp.int32)
    inside = (
        (latitude[None, :] >= band_starts[:, None]) & (latitude[None, :] < band_ends[:, None])
    ).astype(jnp.float32)
    lat_bias = jnp.dot(band_bias, inside, precision=lax.Precision.HIGHEST)
    cell_bias = jnp.broadcast_to(lat_bias[:, :, None], (unit_count, lat_rows, lon_cells)).reshape(
        unit_count, lat_rows * lon_cells
    )
    first_layer = jnp.einsum(
        "hf,bfc->bhc", w_in, rescaled_values, preferred_element_type=jnp.float32
    )
    first_layer = jax.nn.silu(first_layer + cell_bias[None]).astype(jnp.bfloat16)
    second = jnp.einsum("hg,bgc->bhc", w_mid, first_layer, preferred_element_type=jnp.float32)
    second = jax.nn.silu(second).astype(jnp.bfloat16)
    increment = jnp.einsum("fh,bhc->bfc", w_out, second, preferred_element_type=jnp.float32)
    return (values + increment).astype(jnp.bfloat16).reshape(grid_cols.shape)


def local_plain(
    grid_state,
    wave_slots,
    lat_basis,
    vert_modes,
    vert_rates,
    band_sizes,
    norm_gain,
    w_in,
    band_bias,
    w_mid,
    w_out,
):
    members, fields, lev_dev, lat_dev, lon_count = grid_state.shape
    wide_count = lax.axis_size("wide")
    lev_count = lax.axis_size("lev")
    slot_dev, wave_count, lat_count = lat_basis.shape
    levels = lev_dev * lev_count
    padded = extended(grid_state, (("wide", 3),), 1)
    advected = advection_term(padded, grid_state)
    forward, inverse = fourier_tables(wave_slots, lon_count)
    coeffs = jnp.dot(
        advected.reshape(-1, lon_count), forward, preferred_element_type=jnp.float32
    ).astype(jnp.bfloat16)
    coeffs = coeffs.reshape(members, fields, lev_dev, lat_dev, 2, wide_count, lev_count, slot_dev)
    by_wave = lax.all_to_all(
        lax.all_to_all(coeffs, "wide", split_axis=5, concat_axis=3, tiled=True),
        "lev",
        split_axis=6,
        concat_axis=2,
        tiled=True,
    )
    by_wave = by_wave.reshape(members, fields, levels, lat_count, 2, slot_dev)
    block_index = lax.axis_index("wide") * lev_count + lax.axis_index("lev")
    first_slot = block_index * slot_dev
    wave_part = lax.dynamic_slice_in_dim(wave_slots, first_slot, slot_dev)
    raw_spectra = jnp.einsum(
        "skj,bfljrs->sbflrk", lat_basis, by_wave, preferred_element_type=jnp.float32
    )
    spectral = couple(raw_spectra, wave_part, vert_modes, vert_rates)
    rounded = spectral.astype(jnp.bfloat16)
    back_coeffs = jnp.einsum(
        "skj,sbflrk->sbflrj", lat_basis, rounded, preferred_element_type=jnp.float32
    ).astype(jnp.bfloat16)
    lat_quarter = lat_count // (wide_count * lev_count)
    parcel = back_coeffs.reshape(
        1, 1, slot_dev, members, fields, levels, 2, wide_count, lev_count, lat_quarter
    )
    arrived = lax.all_to_all(
        lax.all_to_all(parcel, "wide", split_axis=7, concat_axis=0, tiled=True),
        "lev",
        split_axis=8,
        concat_axis=1,
        tiled=True,
    )
    arrived = arrived.reshape(wave_count, members, fields, levels, 2, lat_quarter)
    grid_mid = jnp.einsum(
        "pbflrj,rpi->bflji", arrived, inverse, preferred_element_type=jnp.float32
    ).astype(jnp.bfloat16)
    new_state = column_net(
        grid_mid, block_index * lat_quarter, band_sizes, norm_gain, w_in, band_bias, w_mid, w_out
    )
    return (spectral, new_state)


LANES = 128
PACK = 16
VMEM_BYTES = 58 * 2**20


FINE = 16


def angle_parts(wave_slots, lon_count):
    coarse = jnp.arange(lon_count // LANES, dtype=jnp.int32) * LANES
    middle = jnp.arange(LANES // FINE, dtype=jnp.int32) * FINE
    fine = jnp.arange(FINE, dtype=jnp.int32)
    longitude = jnp.concatenate([coarse, middle, fine])
    phase = longitude[:, None] * wave_slots[None, :]
    phase = jnp.concatenate([phase, phase + (lon_count - lon_count // 4)], axis=0) % lon_count
    return jnp.cos(phase.astype(jnp.float32) * (2.0 * math.pi / lon_count))


def table_kernel(chunk, parts_ref, out_ref):
    devices, _, per, lon_count = out_ref.shape
    tiles, pieces = lon_count // LANES, LANES // FINE
    count = parts_ref.shape[0] // 2
    apart = parts_ref.shape[1] // devices
    both = parts_ref[...].T
    both = jnp.concatenate(
        [both[d * apart + chunk * per : d * apart + (chunk + 1) * per] for d in range(devices)], axis=0
    )
    cos_parts, sin_parts = both[:, :count], both[:, count:]
    part = lax.broadcasted_iota(jnp.int32, (count, 2 * LANES), 0)
    lane = lax.broadcasted_iota(jnp.int32, (count, 2 * LANES), 1)
    wanted = jnp.where(
        lane < LANES, tiles + lax.div(lane, FINE), tiles + pieces + lax.rem(lane, FINE)
    )
    spread = jnp.where(part == wanted, 1.0, 0.0)
    cos_spread = jnp.dot(cos_parts, spread, precision=lax.Precision.HIGHEST)
    sin_spread = jnp.dot(sin_parts, spread, precision=lax.Precision.HIGHEST)
    cm, cf = cos_spread[:, :LANES], cos_spread[:, LANES:]
    sm, sf = sin_spread[:, :LANES], sin_spread[:, LANES:]
    scale = 1.0 / math.sqrt(lon_count)
    cb, sb = (cm * cf - sm * sf) * scale, (sm * cf + cm * sf) * scale
    for t in range(tiles):
        ca, sa = cos_parts[:, t : t + 1], sin_parts[:, t : t + 1]
        cosine = (ca * cb - sa * sb).astype(jnp.bfloat16)
        minus_sine = (-(sa * cb + ca * sb)).astype(jnp.bfloat16)
        cols = slice(t * LANES, (t + 1) * LANES)
        for d in range(devices):
            out_ref[d, 0, :, cols] = cosine[d * per : (d + 1) * per]
            out_ref[d, 1, :, cols] = minus_sine[d * per : (d + 1) * per]


def table_of(angles, devices, lon_count, chunk, chunks):
    slots = angles.shape[1] // chunks
    return pl.pallas_call(
        functools.partial(table_kernel, chunk),
        out_shape=jax.ShapeDtypeStruct((devices, 2, slots // devices, lon_count), jnp.bfloat16),
        compiler_params=pltpu.CompilerParams(vmem_limit_bytes=VMEM_BYTES),
    )(angles).reshape(2 * slots, lon_count)


def fourier_kernel(x_ref, next_ref, before_ref, after_ref, table_ref, out_ref):
    _, levels, rows, _ = x_ref.shape
    row = lax.broadcasted_iota(jnp.int32, (rows, 1), 0)

    def advected(l):
        x = x_ref[0, l].astype(jnp.float32)
        up = jnp.where(row == rows - 1, after_ref[0, l].astype(jnp.float32), pltpu.roll(x, rows - 1, 0))
        down = jnp.where(row == 0, before_ref[0, l].astype(jnp.float32), pltpu.roll(x, 1, 0))
        mixed = x + transport_speed * next_ref[0, l].astype(jnp.float32) * (up - down)
        return mixed.astype(jnp.bfloat16)

    pair = 2 if levels % 2 == 0 else 1
    for first in range(0, levels, pair):
        both = jnp.concatenate([advected(first + l) for l in range(pair)], axis=0)
        out_ref[:, first * rows : (first + pair) * rows] = lax.dot_general(
            table_ref[...], both, (((1,), (1,)), ((), ())), preferred_element_type=jnp.float32
        ).astype(jnp.bfloat16)


def fourier(grid_state, before, after, table):
    _, fields, lev_dev, lat_dev, lon_count = grid_state.shape
    x, before, after = grid_state[0], before[0], after[0]
    pair = lev_dev if lev_dev <= 4 else 1
    rows = table.shape[0]
    halves = lev_dev // pair
    return pl.pallas_call(
        fourier_kernel,
        grid=(fields, halves),
        in_specs=[
            pl.BlockSpec((1, pair, lat_dev, lon_count), lambda f, h: (f, h, 0, 0)),
            pl.BlockSpec((1, pair, lat_dev, lon_count), lambda f, h: (lax.rem(f + 1, fields), h, 0, 0)),
            pl.BlockSpec((1, pair, 1, lon_count), lambda f, h: (f, h, 0, 0)),
            pl.BlockSpec((1, pair, 1, lon_count), lambda f, h: (f, h, 0, 0)),
            pl.BlockSpec((rows, lon_count), lambda f, h: (0, 0)),
        ],
        out_specs=pl.BlockSpec((rows, pair * lat_dev), lambda f, h: (0, f * halves + h)),
        out_shape=jax.ShapeDtypeStruct((rows, fields * lev_dev * lat_dev), jnp.bfloat16),
        compiler_params=pltpu.CompilerParams(vmem_limit_bytes=VMEM_BYTES),
        cost_estimate=pl.CostEstimate(
            flops=2 * rows * lon_count * fields * lev_dev * lat_dev,
            bytes_accessed=4 * rows * fields * lev_dev * lat_dev,
            transcendentals=0,
        ),
    )(x, x, before, after, table)


def legendre_kernel(
    dims, rates_ref, modes_ref, wave_ref, x_ref, basis_ref, *rest
):
    fields, levels, lev_dev, lev_count, subs, parts = dims
    rest = rest[-len(parts) - 3 :]
    spec_ref, y_refs, (flat_ref, work_ref) = rest[0], rest[1:-2], rest[-2:]
    group, wave_count, lat_count = basis_ref.shape
    cols = fields * 2 * levels
    tiles = lat_count // LANES
    wave_tiles = wave_count // LANES
    wide_count = x_ref.shape[0] // lev_count
    per_tile = lat_count // wide_count // LANES
    jw = LANES // levels

    def place(f, r, l):
        return (f * 2 + r) * levels + l

    for w in range(wide_count):
        for lx in range(lev_count):
            for f in range(fields):
                for l in range(lev_dev):
                    for p in range(per_tile):
                        lane = ((f * lev_dev + l) * per_tile + p) * LANES
                        for r in range(2):
                            block = x_ref[w * lev_count + lx, r, :, lane : lane + LANES].astype(jnp.float32)
                            start = place(f, r, lx * lev_dev + l)
                            for h in range(group // 8):
                                flat_ref[w * per_tile + p, pl.ds(start + h * 8 * cols, 8, stride=cols), :] = block[
                                    h * 8 : (h + 1) * 8
                                ]

    def forward(s, carry):
        rows = pl.ds(pl.multiple_of(s * cols, 8), cols)
        lhs = jnp.concatenate([flat_ref[t, rows, :].astype(jnp.bfloat16) for t in range(tiles)], axis=1)
        raw = lax.dot_general(
            lhs, basis_ref[s], (((1,), (1,)), ((), ())), preferred_element_type=jnp.float32
        )
        for t in range(wave_tiles):
            work_ref[t, rows, :] = raw[:, t * LANES : (t + 1) * LANES]
        return carry

    lax.fori_loop(0, group, forward, 0, unroll=16)

    def couple_tile(step, carry):
        t, h = lax.div(step, group // 8), lax.rem(step, group // 8)
        slot0 = pl.multiple_of(h * 8, 8)
        wave = wave_ref[pl.ds(slot0, 8), :]
        degree = wave + lax.broadcasted_iota(jnp.int32, (8, LANES), 1) + t * LANES
        inside = degree < wave_count
        curvature = (degree * (degree + 1)).astype(jnp.float32) * (1.0 / float(wave_count * wave_count))
        per_slot = fields * levels * wave_tiles * 2

        def gain(f, l):
            return jnp.where(inside, 1.0 / (1.0 + curvature * rates_ref[f, l]), 0.0)

        def where(f, r, l):
            return pl.ds(slot0 * cols + place(f, r, l), 8, stride=cols)

        def keep(f, r, l, value):
            work_ref[t, where(f, r, l), :] = value
            row = ((f * levels + l) * wave_tiles + t) * 2 + r
            spec_ref[pl.ds(slot0 * per_slot + row, 8, stride=per_slot), :] = value

        for l in range(levels):
            scale = gain(0, l)
            for r in range(2):
                keep(0, r, l, work_ref[t, where(0, r, l), :] * scale)
        for f in range(1, fields):
            raw = [[work_ref[t, where(f, r, l), :] for l in range(levels)] for r in range(2)]
            scaled = [[], []]
            for i in range(levels):
                totals = [raw[r][0] * modes_ref[0, i] for r in range(2)]
                for l in range(1, levels):
                    mode = modes_ref[l, i]
                    totals = [totals[r] + raw[r][l] * mode for r in range(2)]
                scale = gain(f, i)
                for r in range(2):
                    scaled[r].append(totals[r] * scale)
            for l in range(levels):
                totals = [scaled[r][0] * modes_ref[l, 0] for r in range(2)]
                for i in range(1, levels):
                    mode = modes_ref[l, i]
                    totals = [totals[r] + scaled[r][i] * mode for r in range(2)]
                for r in range(2):
                    keep(f, r, l, totals[r])
        return carry

    lax.fori_loop(0, wave_tiles * (group // 8), couple_tile, 0)

    def backward(s, carry):
        rows = pl.ds(pl.multiple_of(s * cols, 8), cols)
        lhs = jnp.concatenate(
            [work_ref[t, rows, :].astype(jnp.bfloat16) for t in range(wave_tiles)], axis=1
        )
        back = jnp.dot(lhs, basis_ref[s], preferred_element_type=jnp.float32)
        for t in range(tiles):
            flat_ref[t, rows, :] = back[:, t * LANES : (t + 1) * LANES]
        return carry

    lax.fori_loop(0, group, backward, 0, unroll=16)

    lane = lax.broadcasted_iota(jnp.int32, (8, LANES), 1)
    weights = [
        jnp.where(wave_ref[h * 8 : (h + 1) * 8, :] == 0, 1.0, 2.0) for h in range(group // 8)
    ]
    part_of = {}
    for index, members in enumerate(parts):
        for place_in, sub in enumerate(members):
            part_of[sub] = (index, place_in)
    dest_per_tile = levels // subs if levels >= subs else 1

    def scatter(t, carry):
        for f in range(fields):
            for r in range(2):
                halves = []
                for h in range(group // 8):
                    start = h * 8 * cols
                    pieces = [
                        flat_ref[t, pl.ds(start + place(f, r, l), 8, stride=cols), :] * weights[h]
                        for l in range(levels)
                    ]
                    bit = 1
                    while bit < levels:
                        shift = bit * jw
                        odd = (lane // shift) % 2 == 1
                        swapped = list(pieces)
                        for l in range(levels):
                            if l & bit == 0:
                                low, high = pieces[l], pieces[l | bit]
                                swapped[l] = jnp.where(odd, pltpu.roll(high, shift, 1), low)
                                swapped[l | bit] = jnp.where(odd, high, pltpu.roll(low, LANES - shift, 1))
                        pieces = swapped
                        bit *= 2
                    halves.append(pieces)
                for g in range(levels):
                    block = jnp.concatenate([half[g] for half in halves], axis=0).astype(jnp.bfloat16)
                    index, place_in = part_of[g % subs]
                    y_refs[index][t * dest_per_tile + g // subs, 0, place_in, f, r] = block
        return carry

    lax.fori_loop(0, tiles, scatter, 0)


def legendre(received, lat_basis, wave_part, vert_modes, vert_rates, chunk, so_far, dims):
    fields, levels, lev_dev, lev_count, subs, parts, chunks = dims
    devices = received.shape[0]
    slots, wave_count, lat_count = lat_basis.shape
    group = PACK
    lanes_in = received.shape[-1]
    here = slots // chunks
    steps = here // group
    cols = fields * 2 * levels
    per_slot = fields * levels * (wave_count // LANES) * 2
    args = [vert_rates, vert_modes, wave_part[:, None], received.reshape(devices, 2, here, lanes_in), lat_basis]
    aliases = {}
    if so_far is not None:
        kept = [0] + list(range(2, 1 + len(parts)))
        aliases = {len(args) + n: k for n, k in enumerate(kept)}
        args = args + [so_far[k] for k in kept]
    first = chunk * steps

    def part_spec(index, part):
        block = (devices, 1, len(part), fields, 2, group, LANES)
        if index == 0:
            return pl.BlockSpec(block, lambda g: (0, 0, 0, 0, 0, g, 0))
        return pl.BlockSpec(block, lambda g: (0, chunk, 0, 0, 0, g, 0))

    return pl.pallas_call(
        functools.partial(legendre_kernel, (fields, levels, lev_dev, lev_count, subs, parts)),
        grid=(steps,),
        in_specs=[
            pl.BlockSpec(memory_space=pltpu.SMEM),
            pl.BlockSpec(memory_space=pltpu.SMEM),
            pl.BlockSpec((group, 1), lambda g: (first + g, 0)),
            pl.BlockSpec((devices, 2, group, lanes_in), lambda g: (0, 0, g, 0)),
            pl.BlockSpec((group, wave_count, lat_count), lambda g: (first + g, 0, 0)),
        ]
        + [pl.BlockSpec(memory_space=pl.ANY)] * len(aliases),
        out_specs=[pl.BlockSpec((group * per_slot, LANES), lambda g: (first + g, 0))]
        + [part_spec(i, p) for i, p in enumerate(parts)],
        out_shape=[jax.ShapeDtypeStruct((slots * per_slot, LANES), jnp.float32)]
        + [
            jax.ShapeDtypeStruct(
                (devices, chunks if i else 1, len(p), fields, 2, here, LANES), jnp.bfloat16
            )
            for i, p in enumerate(parts)
        ],
        input_output_aliases=aliases,
        scratch_shapes=[
            pltpu.VMEM((lat_count // LANES, group * cols, LANES), jnp.float32),
            pltpu.VMEM((wave_count // LANES, group * cols, LANES), jnp.float32),
        ],
        compiler_params=pltpu.CompilerParams(vmem_limit_bytes=VMEM_BYTES),
        cost_estimate=pl.CostEstimate(
            flops=40 * here * cols * wave_count * lat_count,
            bytes_accessed=2 * here * wave_count * lat_count,
            transcendentals=0,
        ),
    )(*args)


def column_kernel(
    shape, band_ref, w_in_ref, w_mid_ref, w_out_ref, gain_ref, *rest
):
    fields, levels, jw, padded, chunks, count = shape
    table_refs, y_refs = rest[:chunks], rest[chunks : chunks + count]
    out_ref, grid_ref, done_ref = rest[-3:]
    features = fields * levels
    subs = y_refs[0].shape[2]
    lon_count = table_refs[0].shape[1]
    lon_tiles = lon_count // LANES
    bands = (w_in_ref.shape[1] - padded) // 3
    row = lax.broadcasted_iota(jnp.int32, (3 * bands, lon_count), 0)
    for sub in range(subs):
        pieces = [(y_ref, c) for y_ref in y_refs for c in range(y_ref.shape[1])]
        grid_mid = 0.0
        for (y_ref, c), table_ref in zip(pieces, table_refs):
            lhs = jnp.concatenate([y_ref[:, c, sub, f].reshape(-1, LANES) for f in range(fields)], axis=1)
            grid_mid = grid_mid + lax.dot_general(
                lhs, table_ref[...], (((0,), (0,)), ((), ())), preferred_element_type=jnp.float32
            )
        grid_mid = grid_mid.astype(jnp.bfloat16).astype(jnp.float32)
        for t in range(lon_tiles):
            grid_ref[t] = grid_mid[:, t * LANES : (t + 1) * LANES]

        def one_row(j, carry):
            where = pl.ds(j, features, stride=jw)
            x = jnp.concatenate([grid_ref[t, where, :] for t in range(lon_tiles)], axis=1)
            mean = jnp.sum(x * x, axis=0, keepdims=True) * (1.0 / features)
            normed = x * lax.rsqrt(mean + norm_eps) * gain_ref[...]
            if padded > features:
                normed = jnp.concatenate(
                    [normed, jnp.zeros((padded - features, lon_count), jnp.float32)], axis=0
                )
            chosen = lax.rem(row, bands) == band_ref[sub * jw + j]
            entries = jnp.concatenate(
                [normed.astype(jnp.bfloat16), jnp.where(chosen, 1.0, 0.0).astype(jnp.bfloat16)], axis=0
            )
            half = jnp.dot(w_in_ref[...], entries, preferred_element_type=jnp.float32)
            hidden = (half * jnp.tanh(half) + half).astype(jnp.bfloat16)
            half = jnp.dot(w_mid_ref[...], hidden, preferred_element_type=jnp.float32)
            hidden = (half * jnp.tanh(half) + half).astype(jnp.bfloat16)
            grown = jnp.dot(w_out_ref[...], hidden, preferred_element_type=jnp.float32)
            result = x + grown[:features]
            for t in range(lon_tiles):
                done_ref[t, where, :] = result[:, t * LANES : (t + 1) * LANES]
            return carry

        lax.fori_loop(0, jw, one_row, 0, unroll=4)
        for t in range(lon_tiles):
            out_ref[:, sub * jw : (sub + 1) * jw, t * LANES : (t + 1) * LANES] = (
                done_ref[t].reshape(features, jw, LANES).astype(jnp.bfloat16)
            )


def column_part(arrived, tables, bands_here, weights, so_far, first, lat_quarter, dims):
    fields, levels, jw = dims
    w_in, w_mid, w_out, gain = weights
    padded = w_out.shape[0]
    subs = arrived[0].shape[2]
    features = fields * levels
    depth, lon_count = sum(t.shape[0] for t in tables), tables[0].shape[1]
    rows = subs * jw
    whole = pl.BlockSpec(memory_space=pltpu.VMEM)
    args = [bands_here, w_in, w_mid, w_out, gain] + list(tables) + list(arrived)
    specs = [pl.BlockSpec(memory_space=pltpu.SMEM)] + [whole] * (len(args) - 1)
    aliases = {}
    if so_far is not None:
        args.append(so_far)
        specs.append(pl.BlockSpec(memory_space=pl.ANY))
        aliases = {len(args) - 1: 0}
    block = first // rows
    units = w_mid.shape[0]
    return pl.pallas_call(
        functools.partial(column_kernel, (fields, levels, jw, padded, len(tables), len(arrived))),
        grid=(1,),
        in_specs=specs,
        out_specs=pl.BlockSpec((features, rows, lon_count), lambda g: (0, block, 0)),
        out_shape=jax.ShapeDtypeStruct((features, lat_quarter, lon_count), jnp.bfloat16),
        input_output_aliases=aliases,
        scratch_shapes=[
            pltpu.VMEM((lon_count // LANES, features * jw, LANES), jnp.float32),
            pltpu.VMEM((lon_count // LANES, features * jw, LANES), jnp.float32),
        ],
        compiler_params=pltpu.CompilerParams(vmem_limit_bytes=VMEM_BYTES),
        cost_estimate=pl.CostEstimate(
            flops=2 * rows * lon_count * units * (units + 2 * 256) + 2 * depth * lon_count * features * rows,
            bytes_accessed=4 * features * rows * lon_count,
            transcendentals=2 * rows * lon_count * units,
        ),
    )(*args)


def local_tiled(
    grid_state, wave_slots, lat_basis, vert_modes, vert_rates, band_sizes, norm_gain, w_in, band_bias, w_mid, w_out
):
    _, fields, lev_dev, lat_dev, lon_count = grid_state.shape
    wide_count = lax.axis_size("wide")
    lev_count = lax.axis_size("lev")
    devices = wide_count * lev_count
    slot_dev, wave_count, lat_count = lat_basis.shape
    levels = lev_dev * lev_count
    lat_quarter = lat_count // devices
    jw = LANES // levels
    subs = lat_quarter // jw
    block_index = lax.axis_index("wide") * lev_count + lax.axis_index("lev")

    chunks = 2 if slot_dev % (2 * PACK) == 0 else 1
    angles = angle_parts(wave_slots, lon_count)
    edges = (grid_state[:, :, :, lat_dev - 1 :], grid_state[:, :, :, :1])
    edges, angles = lax.optimization_barrier((edges, angles))
    up = [(i, i + 1) for i in range(wide_count - 1)]
    down = [(j, i) for i, j in up]
    before = lax.ppermute(edges[0], "wide", up)
    after = lax.ppermute(edges[1], "wide", down)
    tables = [table_of(angles, devices, lon_count, c, chunks) for c in range(chunks)]

    def exchange(parcel):
        return lax.all_to_all(parcel, ("wide", "lev"), split_axis=0, concat_axis=0, tiled=True)

    coeffs = [fourier(grid_state, before, after, table) for table in tables]
    received = [exchange(c.reshape(devices, -1, c.shape[1])) for c in coeffs]
    wave_part = lax.dynamic_slice_in_dim(wave_slots, block_index * slot_dev, slot_dev)
    count = 2 if subs % 2 == 0 else 1
    parts = tuple(
        tuple(range(i * subs // count, (i + 1) * subs // count)) for i in range(count)
    )
    dims = (fields, levels, lev_dev, lev_count, subs, parts, chunks)
    bands = band_sizes.shape[0]
    latitude = block_index * lat_quarter + jnp.arange(lat_quarter, dtype=jnp.int32)
    bands_here = jnp.sum(
        (latitude[:, None] >= jnp.cumsum(band_sizes)[None, :]).astype(jnp.int32), axis=1
    )
    features = fields * levels
    padded = -(-features // PACK) * PACK
    pieces, rest = [], band_bias
    for _ in range(3):
        piece = lax.reduce_precision(rest, 8, 7)
        pieces.append(piece.astype(jnp.bfloat16))
        rest = rest - piece
    half = jnp.bfloat16(0.5)
    w_first = jnp.concatenate(
        [jnp.pad(w_in, ((0, 0), (0, padded - features)))] + pieces, axis=1
    ) * half
    weights = (
        w_first,
        w_mid * half,
        jnp.pad(w_out, ((0, padded - features), (0, 0))),
        norm_gain[:, None],
    )
    received[0], weights, bands_here = lax.optimization_barrier((received[0], weights, bands_here))
    so_far, arrived_first = None, []
    for c in range(chunks):
        so_far = legendre(received[c], lat_basis, wave_part, vert_modes, vert_rates, c, so_far, dims)
        parcel = so_far[1]
        if arrived_first:
            arrived_first[-1], parcel = lax.optimization_barrier((arrived_first[-1], parcel))
        arrived_first.append(exchange(parcel))
    spectral = so_far[0].reshape(slot_dev, fields, levels, wave_count // LANES, 2, LANES)
    spectral = spectral.transpose(0, 1, 2, 4, 3, 5).reshape(slot_dev, 1, fields, levels, 2, wave_count)

    new_state = None
    for index, part in enumerate(parts):
        arrived = [exchange(so_far[1 + index])] if index else arrived_first
        rows = slice(part[0] * jw, (part[-1] + 1) * jw)
        new_state = column_part(
            arrived, tables, bands_here[rows], weights, new_state, part[0] * jw, lat_quarter, (fields, levels, jw)
        )
    return spectral, new_state.reshape(1, fields, levels, lat_quarter, lon_count)


def local(grid_state, wave_slots, lat_basis, *rest):
    members, _, lev_dev, lat_dev, lon_count = grid_state.shape
    lev_count = lax.axis_size("lev")
    slot_dev, wave_count, lat_count = lat_basis.shape
    levels = lev_dev * lev_count
    lat_quarter = lat_dev // lev_count
    fits = (
        members == 1
        and levels == 8
        and lat_dev % LANES == 0
        and lon_count % LANES == 0
        and wave_count % LANES == 0
        and slot_dev % PACK == 0
        and lat_quarter % (LANES // levels) == 0
        and lat_quarter <= LANES
    )
    chosen = local_tiled if fits else local_plain
    return chosen(grid_state, wave_slots, lat_basis, *rest)


def solution(mesh):
    placed = (
        P(("groups", "fld"), None, "lev", "wide", None),
        P(),
        P(("wide", "lev"), None, None),
        P(),
        P(),
        P(),
        P(),
        P(),
        P(),
        P(),
        P(),
    )
    return jax.shard_map(
        local,
        mesh=mesh,
        in_specs=placed,
        out_specs=(
            P(("wide", "lev"), ("groups", "fld"), None, None, None, None),
            P(("groups", "fld"), None, None, ("wide", "lev"), None),
        ),
        check_vma=False,
    )
```

```python
import functools
import math

import jax
import jax.numpy as jnp
from jax import lax
from jax.experimental import pallas as pl
from jax.experimental.pallas import tpu as pltpu
from jax.sharding import PartitionSpec as P

transport_speed = 0.5
norm_eps = 1e-06


def extended(array, sides, width):
    for axis, dim in sides:
        size, length = (lax.axis_size(axis), array.shape[dim])
        up = [(i, (i + 1) % size) for i in range(size - 1)]
        down = [(j, i) for i, j in up]
        last = lax.slice_in_dim(array, length - width, length, axis=dim)
        initial = lax.slice_in_dim(array, 0, width, axis=dim)
        before = lax.ppermute(last, axis, up)
        after = lax.ppermute(initial, axis, down)
        array = jnp.concatenate([before, array, after], axis=dim)
    return array


def fourier_tables(wave_slots, lon_count):
    wave_count = wave_slots.shape[0]
    longitude = jnp.arange(lon_count, dtype=jnp.int32)
    integer_phase = longitude[:, None] * wave_slots[None, :] % lon_count
    phase_angle = integer_phase.astype(jnp.float32) * (2.0 * math.pi / lon_count)
    table_scale = 1.0 / math.sqrt(lon_count)
    cosine = jnp.cos(phase_angle) * table_scale
    sine_part = jnp.sin(phase_angle) * table_scale
    forward = (
        jnp.stack([cosine, -sine_part], axis=1)
        .reshape(lon_count, 2 * wave_count)
        .astype(jnp.bfloat16)
    )
    weight = jnp.where(wave_slots == 0, 1.0, 2.0).astype(jnp.float32)
    inverse = jnp.stack(
        [cosine.T * weight[:, None], -sine_part.T * weight[:, None]], axis=0
    ).astype(jnp.bfloat16)
    return (forward, inverse)


def advection_term(padded, main_band_entries):
    above_main_entries = padded[:, :, :, 2:, :].astype(jnp.float32)
    below_main_entries = padded[:, :, :, :-2, :].astype(jnp.float32)
    oscillation_factor = jnp.roll(main_band_entries, -1, axis=1).astype(jnp.float32)
    return (
        main_band_entries.astype(jnp.float32)
        + transport_speed * oscillation_factor * (above_main_entries - below_main_entries)
    ).astype(jnp.bfloat16)


def couple(spectra, wave_part, vert_modes, vert_rates):
    wave_count = spectra.shape[-1]
    degree = wave_part[:, None] + jnp.arange(wave_count, dtype=jnp.int32)[None, :]
    spectra = jnp.where((degree < wave_count)[:, None, None, None, None, :], spectra, 0.0)
    curvature = (degree * (degree + 1)).astype(jnp.float32) / float(wave_count * wave_count)
    vorticity = spectra[:, :, 0] / (
        1.0 + curvature[:, None, None, None, :] * vert_rates[0][None, None, :, None, None]
    )
    coupled_part = spectra[:, :, 1:]
    modal = jnp.einsum(
        "sbflrk,li->sbfirk", coupled_part, vert_modes, precision=lax.Precision.HIGHEST
    )
    scaled = modal / (
        1.0 + curvature[:, None, None, None, None, :] * vert_rates[1:][None, None, :, :, None, None]
    )
    restored = jnp.einsum("sbfirk,li->sbflrk", scaled, vert_modes, precision=lax.Precision.HIGHEST)
    return jnp.concatenate([vorticity[:, :, None], restored], axis=2)


def column_net(grid_cols, lat_first, band_sizes, norm_gain, w_in, band_bias, w_mid, w_out):
    members, fields, levels, lat_rows, lon_cells = grid_cols.shape
    unit_count = w_in.shape[0]
    values = grid_cols.reshape(members, fields * levels, lat_rows * lon_cells).astype(jnp.float32)
    average_squared = jnp.mean(values * values, axis=1, keepdims=True)
    rescaled_values = (
        values * lax.rsqrt(average_squared + norm_eps) * norm_gain[None, :, None]
    ).astype(jnp.bfloat16)
    band_ends = jnp.cumsum(band_sizes)
    band_starts = band_ends - band_sizes
    latitude = lat_first + jnp.arange(lat_rows, dtype=jnp.int32)
    inside = (
        (latitude[None, :] >= band_starts[:, None]) & (latitude[None, :] < band_ends[:, None])
    ).astype(jnp.float32)
    lat_bias = jnp.dot(band_bias, inside, precision=lax.Precision.HIGHEST)
    cell_bias = jnp.broadcast_to(lat_bias[:, :, None], (unit_count, lat_rows, lon_cells)).reshape(
        unit_count, lat_rows * lon_cells
    )
    first_layer = jnp.einsum(
        "hf,bfc->bhc", w_in, rescaled_values, preferred_element_type=jnp.float32
    )
    first_layer = jax.nn.silu(first_layer + cell_bias[None]).astype(jnp.bfloat16)
    second = jnp.einsum("hg,bgc->bhc", w_mid, first_layer, preferred_element_type=jnp.float32)
    second = jax.nn.silu(second).astype(jnp.bfloat16)
    increment = jnp.einsum("fh,bhc->bfc", w_out, second, preferred_element_type=jnp.float32)
    return (values + increment).astype(jnp.bfloat16).reshape(grid_cols.shape)


def local_plain(
    grid_state,
    wave_slots,
    lat_basis,
    vert_modes,
    vert_rates,
    band_sizes,
    norm_gain,
    w_in,
    band_bias,
    w_mid,
    w_out,
):
    members, fields, lev_dev, lat_dev, lon_count = grid_state.shape
    wide_count = lax.axis_size("wide")
    lev_count = lax.axis_size("lev")
    slot_dev, wave_count, lat_count = lat_basis.shape
    levels = lev_dev * lev_count
    padded = extended(grid_state, (("wide", 3),), 1)
    advected = advection_term(padded, grid_state)
    forward, inverse = fourier_tables(wave_slots, lon_count)
    coeffs = jnp.dot(
        advected.reshape(-1, lon_count), forward, preferred_element_type=jnp.float32
    ).astype(jnp.bfloat16)
    coeffs = coeffs.reshape(members, fields, lev_dev, lat_dev, 2, wide_count, lev_count, slot_dev)
    by_wave = lax.all_to_all(
        lax.all_to_all(coeffs, "wide", split_axis=5, concat_axis=3, tiled=True),
        "lev",
        split_axis=6,
        concat_axis=2,
        tiled=True,
    )
    by_wave = by_wave.reshape(members, fields, levels, lat_count, 2, slot_dev)
    block_index = lax.axis_index("wide") * lev_count + lax.axis_index("lev")
    first_slot = block_index * slot_dev
    wave_part = lax.dynamic_slice_in_dim(wave_slots, first_slot, slot_dev)
    raw_spectra = jnp.einsum(
        "skj,bfljrs->sbflrk", lat_basis, by_wave, preferred_element_type=jnp.float32
    )
    spectral = couple(raw_spectra, wave_part, vert_modes, vert_rates)
    rounded = spectral.astype(jnp.bfloat16)
    back_coeffs = jnp.einsum(
        "skj,sbflrk->sbflrj", lat_basis, rounded, preferred_element_type=jnp.float32
    ).astype(jnp.bfloat16)
    lat_quarter = lat_count // (wide_count * lev_count)
    parcel = back_coeffs.reshape(
        1, 1, slot_dev, members, fields, levels, 2, wide_count, lev_count, lat_quarter
    )
    arrived = lax.all_to_all(
        lax.all_to_all(parcel, "wide", split_axis=7, concat_axis=0, tiled=True),
        "lev",
        split_axis=8,
        concat_axis=1,
        tiled=True,
    )
    arrived = arrived.reshape(wave_count, members, fields, levels, 2, lat_quarter)
    grid_mid = jnp.einsum(
        "pbflrj,rpi->bflji", arrived, inverse, preferred_element_type=jnp.float32
    ).astype(jnp.bfloat16)
    new_state = column_net(
        grid_mid, block_index * lat_quarter, band_sizes, norm_gain, w_in, band_bias, w_mid, w_out
    )
    return (spectral, new_state)


LANES = 128
PACK = 16
VMEM_BYTES = 32 * 2**20


FINE = 16


def angle_parts(wave_slots, lon_count):
    coarse = jnp.arange(lon_count // LANES, dtype=jnp.int32) * LANES
    middle = jnp.arange(LANES // FINE, dtype=jnp.int32) * FINE
    fine = jnp.arange(FINE, dtype=jnp.int32)
    longitude = jnp.concatenate([coarse, middle, fine])
    phase = longitude[:, None] * wave_slots[None, :]
    phase = jnp.concatenate([phase, phase + (lon_count - lon_count // 4)], axis=0) % lon_count
    return jnp.cos(phase.astype(jnp.float32) * (2.0 * math.pi / lon_count))


def table_kernel(chunk, parts_ref, out_ref):
    devices, _, per, lon_count = out_ref.shape
    tiles, pieces = lon_count // LANES, LANES // FINE
    count = parts_ref.shape[0] // 2
    apart = parts_ref.shape[1] // devices
    both = parts_ref[...].T
    both = jnp.concatenate(
        [both[d * apart + chunk * per : d * apart + (chunk + 1) * per] for d in range(devices)], axis=0
    )
    cos_parts, sin_parts = both[:, :count], both[:, count:]
    part = lax.broadcasted_iota(jnp.int32, (count, 2 * LANES), 0)
    lane = lax.broadcasted_iota(jnp.int32, (count, 2 * LANES), 1)
    wanted = jnp.where(
        lane < LANES, tiles + lax.div(lane, FINE), tiles + pieces + lax.rem(lane, FINE)
    )
    spread = jnp.where(part == wanted, 1.0, 0.0)
    cos_spread = jnp.dot(cos_parts, spread, precision=lax.Precision.HIGHEST)
    sin_spread = jnp.dot(sin_parts, spread, precision=lax.Precision.HIGHEST)
    cm, cf = cos_spread[:, :LANES], cos_spread[:, LANES:]
    sm, sf = sin_spread[:, :LANES], sin_spread[:, LANES:]
    scale = 1.0 / math.sqrt(lon_count)
    cb, sb = (cm * cf - sm * sf) * scale, (sm * cf + cm * sf) * scale
    for t in range(tiles):
        ca, sa = cos_parts[:, t : t + 1], sin_parts[:, t : t + 1]
        cosine = (ca * cb - sa * sb).astype(jnp.bfloat16)
        minus_sine = (-(sa * cb + ca * sb)).astype(jnp.bfloat16)
        cols = slice(t * LANES, (t + 1) * LANES)
        for d in range(devices):
            out_ref[d, 0, :, cols] = cosine[d * per : (d + 1) * per]
            out_ref[d, 1, :, cols] = minus_sine[d * per : (d + 1) * per]


def table_of(angles, devices, lon_count, chunk, chunks):
    slots = angles.shape[1] // chunks
    return pl.pallas_call(
        functools.partial(table_kernel, chunk),
        out_shape=jax.ShapeDtypeStruct((devices, 2, slots // devices, lon_count), jnp.bfloat16),
        compiler_params=pltpu.CompilerParams(vmem_limit_bytes=VMEM_BYTES),
    )(angles).reshape(2 * slots, lon_count)


def fourier_kernel(x_ref, next_ref, before_ref, after_ref, table_ref, out_ref):
    _, levels, rows, _ = x_ref.shape
    row = lax.broadcasted_iota(jnp.int32, (rows, 1), 0)

    def advected(l):
        x = x_ref[0, l].astype(jnp.float32)
        up = jnp.where(row == rows - 1, after_ref[0, l].astype(jnp.float32), pltpu.roll(x, rows - 1, 0))
        down = jnp.where(row == 0, before_ref[0, l].astype(jnp.float32), pltpu.roll(x, 1, 0))
        mixed = x + transport_speed * next_ref[0, l].astype(jnp.float32) * (up - down)
        return mixed.astype(jnp.bfloat16)

    pair = 2 if levels % 2 == 0 else 1
    for first in range(0, levels, pair):
        both = jnp.concatenate([advected(first + l) for l in range(pair)], axis=0)
        out_ref[:, first * rows : (first + pair) * rows] = lax.dot_general(
            table_ref[...], both, (((1,), (1,)), ((), ())), preferred_element_type=jnp.float32
        ).astype(jnp.bfloat16)


def fourier(grid_state, before, after, table):
    _, fields, lev_dev, lat_dev, lon_count = grid_state.shape
    x, before, after = grid_state[0], before[0], after[0]
    pair = lev_dev if lev_dev <= 4 else 1
    rows = table.shape[0]
    halves = lev_dev // pair
    return pl.pallas_call(
        fourier_kernel,
        grid=(fields, halves),
        in_specs=[
            pl.BlockSpec((1, pair, lat_dev, lon_count), lambda f, h: (f, h, 0, 0)),
            pl.BlockSpec((1, pair, lat_dev, lon_count), lambda f, h: (lax.rem(f + 1, fields), h, 0, 0)),
            pl.BlockSpec((1, pair, 1, lon_count), lambda f, h: (f, h, 0, 0)),
            pl.BlockSpec((1, pair, 1, lon_count), lambda f, h: (f, h, 0, 0)),
            pl.BlockSpec((rows, lon_count), lambda f, h: (0, 0)),
        ],
        out_specs=pl.BlockSpec((rows, pair * lat_dev), lambda f, h: (0, f * halves + h)),
        out_shape=pltpu.HBM((rows, fields * lev_dev * lat_dev), jnp.bfloat16),
        compiler_params=pltpu.CompilerParams(vmem_limit_bytes=VMEM_BYTES),
        cost_estimate=pl.CostEstimate(
            flops=2 * rows * lon_count * fields * lev_dev * lat_dev,
            bytes_accessed=4 * rows * fields * lev_dev * lat_dev,
            transcendentals=0,
        ),
    )(x, x, before, after, table)


def legendre_kernel(
    dims, rates_ref, modes_ref, wave_ref, x_ref, basis_ref, *rest
):
    fields, levels, lev_dev, lev_count, subs, parts = dims
    rest = rest[-len(parts) - 3 :]
    spec_ref, y_refs, (flat_ref, work_ref) = rest[0], rest[1:-2], rest[-2:]
    group, wave_count, lat_count = basis_ref.shape
    cols = fields * 2 * levels
    tiles = lat_count // LANES
    wave_tiles = wave_count // LANES
    wide_count = x_ref.shape[0] // lev_count
    per_tile = lat_count // wide_count // LANES
    jw = LANES // levels

    def place(f, r, l):
        return (f * 2 + r) * levels + l

    for w in range(wide_count):
        for lx in range(lev_count):
            for f in range(fields):
                for l in range(lev_dev):
                    for p in range(per_tile):
                        lane = ((f * lev_dev + l) * per_tile + p) * LANES
                        for r in range(2):
                            block = x_ref[w * lev_count + lx, r, :, lane : lane + LANES].astype(jnp.float32)
                            start = place(f, r, lx * lev_dev + l)
                            for h in range(group // 8):
                                flat_ref[w * per_tile + p, pl.ds(start + h * 8 * cols, 8, stride=cols), :] = block[
                                    h * 8 : (h + 1) * 8
                                ]

    def forward(s, carry):
        rows = pl.ds(pl.multiple_of(s * cols, 8), cols)
        lhs = jnp.concatenate([flat_ref[t, rows, :].astype(jnp.bfloat16) for t in range(tiles)], axis=1)
        raw = lax.dot_general(
            lhs, basis_ref[s], (((1,), (1,)), ((), ())), preferred_element_type=jnp.float32
        )
        for t in range(wave_tiles):
            work_ref[t, rows, :] = raw[:, t * LANES : (t + 1) * LANES]
        return carry

    lax.fori_loop(0, group, forward, 0, unroll=16)

    def couple_tile(step, carry):
        t, h = lax.div(step, group // 8), lax.rem(step, group // 8)
        slot0 = pl.multiple_of(h * 8, 8)
        wave = wave_ref[pl.ds(slot0, 8), :]
        degree = wave + lax.broadcasted_iota(jnp.int32, (8, LANES), 1) + t * LANES
        inside = degree < wave_count
        curvature = (degree * (degree + 1)).astype(jnp.float32) * (1.0 / float(wave_count * wave_count))
        per_slot = fields * levels * wave_tiles * 2

        def gain(f, l):
            return jnp.where(inside, 1.0 / (1.0 + curvature * rates_ref[f, l]), 0.0)

        def where(f, r, l):
            return pl.ds(slot0 * cols + place(f, r, l), 8, stride=cols)

        def keep(f, r, l, value):
            work_ref[t, where(f, r, l), :] = value
            row = ((f * levels + l) * wave_tiles + t) * 2 + r
            spec_ref[pl.ds(slot0 * per_slot + row, 8, stride=per_slot), :] = value

        for l in range(levels):
            scale = gain(0, l)
            for r in range(2):
                keep(0, r, l, work_ref[t, where(0, r, l), :] * scale)
        for f in range(1, fields):
            raw = [[work_ref[t, where(f, r, l), :] for l in range(levels)] for r in range(2)]
            scaled = [[], []]
            for i in range(levels):
                totals = [raw[r][0] * modes_ref[0, i] for r in range(2)]
                for l in range(1, levels):
                    mode = modes_ref[l, i]
                    totals = [totals[r] + raw[r][l] * mode for r in range(2)]
                scale = gain(f, i)
                for r in range(2):
                    scaled[r].append(totals[r] * scale)
            for l in range(levels):
                totals = [scaled[r][0] * modes_ref[l, 0] for r in range(2)]
                for i in range(1, levels):
                    mode = modes_ref[l, i]
                    totals = [totals[r] + scaled[r][i] * mode for r in range(2)]
                for r in range(2):
                    keep(f, r, l, totals[r])
        return carry

    lax.fori_loop(0, wave_tiles * (group // 8), couple_tile, 0)

    def backward(s, carry):
        rows = pl.ds(pl.multiple_of(s * cols, 8), cols)
        lhs = jnp.concatenate(
            [work_ref[t, rows, :].astype(jnp.bfloat16) for t in range(wave_tiles)], axis=1
        )
        back = jnp.dot(lhs, basis_ref[s], preferred_element_type=jnp.float32)
        for t in range(tiles):
            flat_ref[t, rows, :] = back[:, t * LANES : (t + 1) * LANES]
        return carry

    lax.fori_loop(0, group, backward, 0, unroll=16)

    lane = lax.broadcasted_iota(jnp.int32, (8, LANES), 1)
    weights = [
        jnp.where(wave_ref[h * 8 : (h + 1) * 8, :] == 0, 1.0, 2.0) for h in range(group // 8)
    ]
    part_of = {}
    for index, members in enumerate(parts):
        for place_in, sub in enumerate(members):
            part_of[sub] = (index, place_in)
    dest_per_tile = levels // subs if levels >= subs else 1

    def scatter(t, carry):
        for f in range(fields):
            for r in range(2):
                halves = []
                for h in range(group // 8):
                    start = h * 8 * cols
                    pieces = [
                        flat_ref[t, pl.ds(start + place(f, r, l), 8, stride=cols), :] * weights[h]
                        for l in range(levels)
                    ]
                    bit = 1
                    while bit < levels:
                        shift = bit * jw
                        odd = (lane // shift) % 2 == 1
                        swapped = list(pieces)
                        for l in range(levels):
                            if l & bit == 0:
                                low, high = pieces[l], pieces[l | bit]
                                swapped[l] = jnp.where(odd, pltpu.roll(high, shift, 1), low)
                                swapped[l | bit] = jnp.where(odd, high, pltpu.roll(low, LANES - shift, 1))
                        pieces = swapped
                        bit *= 2
                    halves.append(pieces)
                for g in range(levels):
                    block = jnp.concatenate([half[g] for half in halves], axis=0).astype(jnp.bfloat16)
                    index, place_in = part_of[g % subs]
                    y_refs[index][t * dest_per_tile + g // subs, 0, place_in, f, r] = block
        return carry

    lax.fori_loop(0, tiles, scatter, 0)


def legendre(received, lat_basis, wave_part, vert_modes, vert_rates, chunk, so_far, dims):
    fields, levels, lev_dev, lev_count, subs, parts, chunks = dims
    devices = received.shape[0]
    slots, wave_count, lat_count = lat_basis.shape
    group = PACK
    lanes_in = received.shape[-1]
    here = slots // chunks
    steps = here // group
    cols = fields * 2 * levels
    per_slot = fields * levels * (wave_count // LANES) * 2
    args = [vert_rates, vert_modes, wave_part[:, None], received.reshape(devices, 2, here, lanes_in), lat_basis]
    aliases = {}
    if so_far is not None:
        kept = [0] + list(range(2, 1 + len(parts)))
        aliases = {len(args) + n: k for n, k in enumerate(kept)}
        args = args + [so_far[k] for k in kept]
    first = chunk * steps

    def part_spec(index, part):
        block = (devices, 1, len(part), fields, 2, group, LANES)
        if index == 0:
            return pl.BlockSpec(block, lambda g: (0, 0, 0, 0, 0, g, 0))
        return pl.BlockSpec(block, lambda g: (0, chunk, 0, 0, 0, g, 0))

    return pl.pallas_call(
        functools.partial(legendre_kernel, (fields, levels, lev_dev, lev_count, subs, parts)),
        grid=(steps,),
        in_specs=[
            pl.BlockSpec(memory_space=pltpu.SMEM),
            pl.BlockSpec(memory_space=pltpu.SMEM),
            pl.BlockSpec((group, 1), lambda g: (first + g, 0)),
            pl.BlockSpec((devices, 2, group, lanes_in), lambda g: (0, 0, g, 0)),
            pl.BlockSpec((group, wave_count, lat_count), lambda g: (first + g, 0, 0)),
        ]
        + [pl.BlockSpec(memory_space=pl.ANY)] * len(aliases),
        out_specs=[pl.BlockSpec((group * per_slot, LANES), lambda g: (first + g, 0))]
        + [part_spec(i, p) for i, p in enumerate(parts)],
        out_shape=[pltpu.HBM((slots * per_slot, LANES), jnp.float32)]
        + [
            pltpu.HBM(
                (devices, chunks if i else 1, len(p), fields, 2, here, LANES), jnp.bfloat16
            )
            for i, p in enumerate(parts)
        ],
        input_output_aliases=aliases,
        scratch_shapes=[
            pltpu.VMEM((lat_count // LANES, group * cols, LANES), jnp.float32),
            pltpu.VMEM((wave_count // LANES, group * cols, LANES), jnp.float32),
        ],
        compiler_params=pltpu.CompilerParams(vmem_limit_bytes=VMEM_BYTES),
        cost_estimate=pl.CostEstimate(
            flops=40 * here * cols * wave_count * lat_count,
            bytes_accessed=2 * here * wave_count * lat_count,
            transcendentals=0,
        ),
    )(*args)


def column_kernel(
    shape, scalars_ref, w_in_ref, w_deep_ref, *rest
):
    fields, levels, jw, padded, chunks, count = shape
    table_refs, y_refs = rest[:chunks], rest[chunks : chunks + count]
    out_ref, grid_ref, done_ref, gain_ref = rest[-4:]
    features = fields * levels
    for i in range(features):
        gain_ref[i : i + 1, :] = jnp.full((1, LANES), scalars_ref[i])
    subs = y_refs[0].shape[2]
    lon_count = table_refs[0].shape[1]
    lon_tiles = lon_count // LANES
    bands = (w_in_ref.shape[1] - padded) // 3
    row = lax.rem(lax.broadcasted_iota(jnp.int32, (3 * bands, lon_count), 0), bands).astype(jnp.float32)
    units = w_in_ref.shape[0]
    gain = jnp.concatenate([gain_ref[...]] * lon_tiles, axis=1)
    for sub in range(subs):
        pieces = [(y_ref, c) for y_ref in y_refs for c in range(y_ref.shape[1])]
        grid_mid = 0.0
        for (y_ref, c), table_ref in zip(pieces, table_refs):
            lhs = jnp.concatenate([y_ref[:, c, sub, f].reshape(-1, LANES) for f in range(fields)], axis=1)
            grid_mid = grid_mid + lax.dot_general(
                lhs, table_ref[...], (((0,), (0,)), ((), ())), preferred_element_type=jnp.float32
            )
        grid_mid = grid_mid.astype(jnp.bfloat16).astype(jnp.float32)
        for t in range(lon_tiles):
            grid_ref[t] = grid_mid[:, t * LANES : (t + 1) * LANES]

        def one_row(j, carry):
            where = pl.ds(j, features, stride=jw)
            x = jnp.concatenate([grid_ref[t, where, :] for t in range(lon_tiles)], axis=1)
            mean = jnp.sum(x * x, axis=0, keepdims=True) * (1.0 / features)
            normed = x * lax.rsqrt(mean + norm_eps) * gain
            if padded > features:
                normed = jnp.concatenate(
                    [normed, jnp.zeros((padded - features, lon_count), jnp.float32)], axis=0
                )
            chosen = row == scalars_ref[features + sub * jw + j]
            entries = jnp.concatenate(
                [normed.astype(jnp.bfloat16), jnp.where(chosen, 1.0, 0.0).astype(jnp.bfloat16)], axis=0
            )
            half = jnp.dot(w_in_ref[...], entries, preferred_element_type=jnp.float32)
            hidden = (half * jnp.tanh(half) + half).astype(jnp.bfloat16)
            half = jnp.dot(w_deep_ref[:units], hidden, preferred_element_type=jnp.float32)
            hidden = (half * jnp.tanh(half) + half).astype(jnp.bfloat16)
            grown = jnp.dot(w_deep_ref[units:], hidden, preferred_element_type=jnp.float32)
            result = x + grown[:features]
            for t in range(lon_tiles):
                done_ref[t, where, :] = result[:, t * LANES : (t + 1) * LANES]
            return carry

        lax.fori_loop(0, jw, one_row, 0, unroll=4)
        for t in range(lon_tiles):
            out_ref[:, sub * jw : (sub + 1) * jw, t * LANES : (t + 1) * LANES] = (
                done_ref[t].reshape(features, jw, LANES).astype(jnp.bfloat16)
            )


def column_part(arrived, tables, bands_here, weights, so_far, first, lat_quarter, dims):
    fields, levels, jw = dims
    w_in, w_deep, gain = weights
    units = w_in.shape[0]
    padded = w_deep.shape[0] - units
    scalars = jnp.concatenate([gain, bands_here.astype(jnp.float32)])
    subs = arrived[0].shape[2]
    features = fields * levels
    depth, lon_count = sum(t.shape[0] for t in tables), tables[0].shape[1]
    rows = subs * jw
    whole = pl.BlockSpec(memory_space=pltpu.VMEM)
    args = [scalars, w_in, w_deep] + list(tables) + list(arrived)
    specs = [pl.BlockSpec(memory_space=pltpu.SMEM)] + [whole] * (len(args) - 1)
    aliases = {}
    if so_far is not None:
        args.append(so_far)
        specs.append(pl.BlockSpec(memory_space=pl.ANY))
        aliases = {len(args) - 1: 0}
    block = first // rows
    return pl.pallas_call(
        functools.partial(column_kernel, (fields, levels, jw, padded, len(tables), len(arrived))),
        grid=(1,),
        in_specs=specs,
        out_specs=pl.BlockSpec((features, rows, lon_count), lambda g: (0, block, 0)),
        out_shape=jax.ShapeDtypeStruct((features, lat_quarter, lon_count), jnp.bfloat16),
        input_output_aliases=aliases,
        scratch_shapes=[
            pltpu.VMEM((lon_count // LANES, features * jw, LANES), jnp.float32),
            pltpu.VMEM((lon_count // LANES, features * jw, LANES), jnp.float32),
            pltpu.VMEM((features, LANES), jnp.float32),
        ],
        compiler_params=pltpu.CompilerParams(vmem_limit_bytes=VMEM_BYTES),
        cost_estimate=pl.CostEstimate(
            flops=2 * rows * lon_count * units * (units + 2 * 256) + 2 * depth * lon_count * features * rows,
            bytes_accessed=4 * features * rows * lon_count,
            transcendentals=2 * rows * lon_count * units,
        ),
    )(*args)


def local_tiled(
    grid_state, wave_slots, lat_basis, vert_modes, vert_rates, band_sizes, norm_gain, w_in, band_bias, w_mid, w_out
):
    _, fields, lev_dev, lat_dev, lon_count = grid_state.shape
    wide_count = lax.axis_size("wide")
    lev_count = lax.axis_size("lev")
    devices = wide_count * lev_count
    slot_dev, wave_count, lat_count = lat_basis.shape
    levels = lev_dev * lev_count
    lat_quarter = lat_count // devices
    jw = LANES // levels
    subs = lat_quarter // jw
    block_index = lax.axis_index("wide") * lev_count + lax.axis_index("lev")

    chunks = 2 if slot_dev % (2 * PACK) == 0 else 1
    angles = angle_parts(wave_slots, lon_count)
    edges = (grid_state[:, :, :, lat_dev - 1 :], grid_state[:, :, :, :1])
    up = [(i, i + 1) for i in range(wide_count - 1)]
    down = [(j, i) for i, j in up]
    before = lax.ppermute(edges[0], "wide", up)
    after = lax.ppermute(edges[1], "wide", down)
    tables = [table_of(angles, devices, lon_count, c, chunks) for c in range(chunks)]

    def exchange(parcel):
        return lax.all_to_all(parcel, ("wide", "lev"), split_axis=0, concat_axis=0, tiled=True)

    coeffs = [fourier(grid_state, before, after, table) for table in tables]
    received = [exchange(c.reshape(devices, -1, c.shape[1])) for c in coeffs]
    wave_part = lax.dynamic_slice_in_dim(wave_slots, block_index * slot_dev, slot_dev)
    count = 2 if subs % 2 == 0 else 1
    parts = tuple(
        tuple(range(i * subs // count, (i + 1) * subs // count)) for i in range(count)
    )
    dims = (fields, levels, lev_dev, lev_count, subs, parts, chunks)
    bands = band_sizes.shape[0]
    latitude = block_index * lat_quarter + jnp.arange(lat_quarter, dtype=jnp.int32)
    bands_here = jnp.sum(
        (latitude[:, None] >= jnp.cumsum(band_sizes)[None, :]).astype(jnp.int32), axis=1
    )
    features = fields * levels
    padded = -(-features // PACK) * PACK
    pieces, rest = [], band_bias
    for _ in range(3):
        piece = lax.reduce_precision(rest, 8, 7)
        pieces.append(piece.astype(jnp.bfloat16))
        rest = rest - piece
    half = jnp.bfloat16(0.5)
    w_first = jnp.concatenate(
        [jnp.pad(w_in, ((0, 0), (0, padded - features)))] + pieces, axis=1
    ) * half
    weights = (
        w_first,
        jnp.concatenate([w_mid * half, jnp.pad(w_out, ((0, padded - features), (0, 0)))], axis=0),
        norm_gain,
    )
    received[0], weights, bands_here = lax.optimization_barrier((received[0], weights, bands_here))
    so_far, arrived_first = None, []
    for c in range(chunks):
        so_far = legendre(received[c], lat_basis, wave_part, vert_modes, vert_rates, c, so_far, dims)
        parcel = so_far[1]
        if arrived_first:
            arrived_first[-1], parcel = lax.optimization_barrier((arrived_first[-1], parcel))
        arrived_first.append(exchange(parcel))
    spectral = so_far[0].reshape(slot_dev, fields, levels, wave_count // LANES, 2, LANES)
    spectral = spectral.transpose(0, 1, 2, 4, 3, 5).reshape(slot_dev, 1, fields, levels, 2, wave_count)

    new_state = None
    for index, part in enumerate(parts):
        arrived = [exchange(so_far[1 + index])] if index else arrived_first
        rows = slice(part[0] * jw, (part[-1] + 1) * jw)
        new_state = column_part(
            arrived, tables, bands_here[rows], weights, new_state, part[0] * jw, lat_quarter, (fields, levels, jw)
        )
    return spectral, new_state.reshape(1, fields, levels, lat_quarter, lon_count)


def local(grid_state, wave_slots, lat_basis, *rest):
    members, _, lev_dev, lat_dev, lon_count = grid_state.shape
    lev_count = lax.axis_size("lev")
    slot_dev, wave_count, lat_count = lat_basis.shape
    levels = lev_dev * lev_count
    lat_quarter = lat_dev // lev_count
    fits = (
        members == 1
        and levels == 8
        and lat_dev % LANES == 0
        and lon_count % LANES == 0
        and wave_count % LANES == 0
        and slot_dev % PACK == 0
        and lat_quarter % (LANES // levels) == 0
        and lat_quarter <= LANES
    )
    chosen = local_tiled if fits else local_plain
    return chosen(grid_state, wave_slots, lat_basis, *rest)


def solution(mesh):
    placed = (
        P(("groups", "fld"), None, "lev", "wide", None),
        P(),
        P(("wide", "lev"), None, None),
        P(),
        P(),
        P(),
        P(),
        P(),
        P(),
        P(),
        P(),
    )
    return jax.shard_map(
        local,
        mesh=mesh,
        in_specs=placed,
        out_specs=(
            P(("wide", "lev"), ("groups", "fld"), None, None, None, None),
            P(("groups", "fld"), None, None, ("wide", "lev"), None),
        ),
        check_vma=False,
    )
```

```python
import functools
import math

import jax
import jax.numpy as jnp
from jax import lax
from jax.experimental import pallas as pl
from jax.experimental.pallas import tpu as pltpu
from jax.sharding import PartitionSpec as P

transport_speed = 0.5
norm_eps = 1e-06


def extended(array, sides, width):
    for axis, dim in sides:
        size, length = (lax.axis_size(axis), array.shape[dim])
        up = [(i, (i + 1) % size) for i in range(size - 1)]
        down = [(j, i) for i, j in up]
        last = lax.slice_in_dim(array, length - width, length, axis=dim)
        initial = lax.slice_in_dim(array, 0, width, axis=dim)
        before = lax.ppermute(last, axis, up)
        after = lax.ppermute(initial, axis, down)
        array = jnp.concatenate([before, array, after], axis=dim)
    return array


def fourier_tables(wave_slots, lon_count):
    wave_count = wave_slots.shape[0]
    longitude = jnp.arange(lon_count, dtype=jnp.int32)
    integer_phase = longitude[:, None] * wave_slots[None, :] % lon_count
    phase_angle = integer_phase.astype(jnp.float32) * (2.0 * math.pi / lon_count)
    table_scale = 1.0 / math.sqrt(lon_count)
    cosine = jnp.cos(phase_angle) * table_scale
    sine_part = jnp.sin(phase_angle) * table_scale
    forward = (
        jnp.stack([cosine, -sine_part], axis=1)
        .reshape(lon_count, 2 * wave_count)
        .astype(jnp.bfloat16)
    )
    weight = jnp.where(wave_slots == 0, 1.0, 2.0).astype(jnp.float32)
    inverse = jnp.stack(
        [cosine.T * weight[:, None], -sine_part.T * weight[:, None]], axis=0
    ).astype(jnp.bfloat16)
    return (forward, inverse)


def advection_term(padded, main_band_entries):
    above_main_entries = padded[:, :, :, 2:, :].astype(jnp.float32)
    below_main_entries = padded[:, :, :, :-2, :].astype(jnp.float32)
    oscillation_factor = jnp.roll(main_band_entries, -1, axis=1).astype(jnp.float32)
    return (
        main_band_entries.astype(jnp.float32)
        + transport_speed * oscillation_factor * (above_main_entries - below_main_entries)
    ).astype(jnp.bfloat16)


def couple(spectra, wave_part, vert_modes, vert_rates):
    wave_count = spectra.shape[-1]
    degree = wave_part[:, None] + jnp.arange(wave_count, dtype=jnp.int32)[None, :]
    spectra = jnp.where((degree < wave_count)[:, None, None, None, None, :], spectra, 0.0)
    curvature = (degree * (degree + 1)).astype(jnp.float32) / float(wave_count * wave_count)
    vorticity = spectra[:, :, 0] / (
        1.0 + curvature[:, None, None, None, :] * vert_rates[0][None, None, :, None, None]
    )
    coupled_part = spectra[:, :, 1:]
    modal = jnp.einsum(
        "sbflrk,li->sbfirk", coupled_part, vert_modes, precision=lax.Precision.HIGHEST
    )
    scaled = modal / (
        1.0 + curvature[:, None, None, None, None, :] * vert_rates[1:][None, None, :, :, None, None]
    )
    restored = jnp.einsum("sbfirk,li->sbflrk", scaled, vert_modes, precision=lax.Precision.HIGHEST)
    return jnp.concatenate([vorticity[:, :, None], restored], axis=2)


def column_net(grid_cols, lat_first, band_sizes, norm_gain, w_in, band_bias, w_mid, w_out):
    members, fields, levels, lat_rows, lon_cells = grid_cols.shape
    unit_count = w_in.shape[0]
    values = grid_cols.reshape(members, fields * levels, lat_rows * lon_cells).astype(jnp.float32)
    average_squared = jnp.mean(values * values, axis=1, keepdims=True)
    rescaled_values = (
        values * lax.rsqrt(average_squared + norm_eps) * norm_gain[None, :, None]
    ).astype(jnp.bfloat16)
    band_ends = jnp.cumsum(band_sizes)
    band_starts = band_ends - band_sizes
    latitude = lat_first + jnp.arange(lat_rows, dtype=jnp.int32)
    inside = (
        (latitude[None, :] >= band_starts[:, None]) & (latitude[None, :] < band_ends[:, None])
    ).astype(jnp.float32)
    lat_bias = jnp.dot(band_bias, inside, precision=lax.Precision.HIGHEST)
    cell_bias = jnp.broadcast_to(lat_bias[:, :, None], (unit_count, lat_rows, lon_cells)).reshape(
        unit_count, lat_rows * lon_cells
    )
    first_layer = jnp.einsum(
        "hf,bfc->bhc", w_in, rescaled_values, preferred_element_type=jnp.float32
    )
    first_layer = jax.nn.silu(first_layer + cell_bias[None]).astype(jnp.bfloat16)
    second = jnp.einsum("hg,bgc->bhc", w_mid, first_layer, preferred_element_type=jnp.float32)
    second = jax.nn.silu(second).astype(jnp.bfloat16)
    increment = jnp.einsum("fh,bhc->bfc", w_out, second, preferred_element_type=jnp.float32)
    return (values + increment).astype(jnp.bfloat16).reshape(grid_cols.shape)


def local_plain(
    grid_state,
    wave_slots,
    lat_basis,
    vert_modes,
    vert_rates,
    band_sizes,
    norm_gain,
    w_in,
    band_bias,
    w_mid,
    w_out,
):
    members, fields, lev_dev, lat_dev, lon_count = grid_state.shape
    wide_count = lax.axis_size("wide")
    lev_count = lax.axis_size("lev")
    slot_dev, wave_count, lat_count = lat_basis.shape
    levels = lev_dev * lev_count
    padded = extended(grid_state, (("wide", 3),), 1)
    advected = advection_term(padded, grid_state)
    forward, inverse = fourier_tables(wave_slots, lon_count)
    coeffs = jnp.dot(
        advected.reshape(-1, lon_count), forward, preferred_element_type=jnp.float32
    ).astype(jnp.bfloat16)
    coeffs = coeffs.reshape(members, fields, lev_dev, lat_dev, 2, wide_count, lev_count, slot_dev)
    by_wave = lax.all_to_all(
        lax.all_to_all(coeffs, "wide", split_axis=5, concat_axis=3, tiled=True),
        "lev",
        split_axis=6,
        concat_axis=2,
        tiled=True,
    )
    by_wave = by_wave.reshape(members, fields, levels, lat_count, 2, slot_dev)
    block_index = lax.axis_index("wide") * lev_count + lax.axis_index("lev")
    first_slot = block_index * slot_dev
    wave_part = lax.dynamic_slice_in_dim(wave_slots, first_slot, slot_dev)
    raw_spectra = jnp.einsum(
        "skj,bfljrs->sbflrk", lat_basis, by_wave, preferred_element_type=jnp.float32
    )
    spectral = couple(raw_spectra, wave_part, vert_modes, vert_rates)
    rounded = spectral.astype(jnp.bfloat16)
    back_coeffs = jnp.einsum(
        "skj,sbflrk->sbflrj", lat_basis, rounded, preferred_element_type=jnp.float32
    ).astype(jnp.bfloat16)
    lat_quarter = lat_count // (wide_count * lev_count)
    parcel = back_coeffs.reshape(
        1, 1, slot_dev, members, fields, levels, 2, wide_count, lev_count, lat_quarter
    )
    arrived = lax.all_to_all(
        lax.all_to_all(parcel, "wide", split_axis=7, concat_axis=0, tiled=True),
        "lev",
        split_axis=8,
        concat_axis=1,
        tiled=True,
    )
    arrived = arrived.reshape(wave_count, members, fields, levels, 2, lat_quarter)
    grid_mid = jnp.einsum(
        "pbflrj,rpi->bflji", arrived, inverse, preferred_element_type=jnp.float32
    ).astype(jnp.bfloat16)
    new_state = column_net(
        grid_mid, block_index * lat_quarter, band_sizes, norm_gain, w_in, band_bias, w_mid, w_out
    )
    return (spectral, new_state)


LANES = 128
PACK = 16
VMEM_BYTES = 32 * 2**20


FINE = 16


def angle_parts(wave_slots, lon_count):
    coarse = jnp.arange(lon_count // LANES, dtype=jnp.int32) * LANES
    middle = jnp.arange(LANES // FINE, dtype=jnp.int32) * FINE
    fine = jnp.arange(FINE, dtype=jnp.int32)
    longitude = jnp.concatenate([coarse, middle, fine])
    phase = longitude[:, None] * wave_slots[None, :]
    phase = jnp.concatenate([phase, phase + (lon_count - lon_count // 4)], axis=0) % lon_count
    return jnp.cos(phase.astype(jnp.float32) * (2.0 * math.pi / lon_count))


def table_kernel(chunk, parts_ref, out_ref):
    devices, _, per, lon_count = out_ref.shape
    tiles, pieces = lon_count // LANES, LANES // FINE
    count = parts_ref.shape[0] // 2
    apart = parts_ref.shape[1] // devices
    both = parts_ref[...].T
    both = jnp.concatenate(
        [both[d * apart + chunk * per : d * apart + (chunk + 1) * per] for d in range(devices)], axis=0
    )
    cos_parts, sin_parts = both[:, :count], both[:, count:]
    part = lax.broadcasted_iota(jnp.int32, (count, 2 * LANES), 0)
    lane = lax.broadcasted_iota(jnp.int32, (count, 2 * LANES), 1)
    wanted = jnp.where(
        lane < LANES, tiles + lax.div(lane, FINE), tiles + pieces + lax.rem(lane, FINE)
    )
    spread = jnp.where(part == wanted, 1.0, 0.0)
    cos_spread = jnp.dot(cos_parts, spread, precision=lax.Precision.HIGHEST)
    sin_spread = jnp.dot(sin_parts, spread, precision=lax.Precision.HIGHEST)
    cm, cf = cos_spread[:, :LANES], cos_spread[:, LANES:]
    sm, sf = sin_spread[:, :LANES], sin_spread[:, LANES:]
    scale = 1.0 / math.sqrt(lon_count)
    cb, sb = (cm * cf - sm * sf) * scale, (sm * cf + cm * sf) * scale
    for t in range(tiles):
        ca, sa = cos_parts[:, t : t + 1], sin_parts[:, t : t + 1]
        cosine = (ca * cb - sa * sb).astype(jnp.bfloat16)
        minus_sine = (-(sa * cb + ca * sb)).astype(jnp.bfloat16)
        cols = slice(t * LANES, (t + 1) * LANES)
        for d in range(devices):
            out_ref[d, 0, :, cols] = cosine[d * per : (d + 1) * per]
            out_ref[d, 1, :, cols] = minus_sine[d * per : (d + 1) * per]


def table_of(angles, devices, lon_count, chunk, chunks):
    slots = angles.shape[1] // chunks
    return pl.pallas_call(
        functools.partial(table_kernel, chunk),
        out_shape=jax.ShapeDtypeStruct((devices, 2, slots // devices, lon_count), jnp.bfloat16),
        compiler_params=pltpu.CompilerParams(vmem_limit_bytes=VMEM_BYTES),
    )(angles).reshape(2 * slots, lon_count)


def fourier_kernel(x_ref, next_ref, before_ref, after_ref, table_ref, out_ref):
    _, levels, rows, _ = x_ref.shape
    row = lax.broadcasted_iota(jnp.int32, (rows, 1), 0)

    def advected(l):
        x = x_ref[0, l].astype(jnp.float32)
        up = jnp.where(row == rows - 1, after_ref[0, l].astype(jnp.float32), pltpu.roll(x, rows - 1, 0))
        down = jnp.where(row == 0, before_ref[0, l].astype(jnp.float32), pltpu.roll(x, 1, 0))
        mixed = x + transport_speed * next_ref[0, l].astype(jnp.float32) * (up - down)
        return mixed.astype(jnp.bfloat16)

    pair = 2 if levels % 2 == 0 else 1
    for first in range(0, levels, pair):
        both = jnp.concatenate([advected(first + l) for l in range(pair)], axis=0)
        out_ref[:, first * rows : (first + pair) * rows] = lax.dot_general(
            table_ref[...], both, (((1,), (1,)), ((), ())), preferred_element_type=jnp.float32
        ).astype(jnp.bfloat16)


def fourier(grid_state, before, after, table):
    _, fields, lev_dev, lat_dev, lon_count = grid_state.shape
    x, before, after = grid_state[0], before[0], after[0]
    pair = lev_dev if lev_dev <= 4 else 1
    rows = table.shape[0]
    halves = lev_dev // pair
    return pl.pallas_call(
        fourier_kernel,
        grid=(fields, halves),
        in_specs=[
            pl.BlockSpec((1, pair, lat_dev, lon_count), lambda f, h: (f, h, 0, 0)),
            pl.BlockSpec((1, pair, lat_dev, lon_count), lambda f, h: (lax.rem(f + 1, fields), h, 0, 0)),
            pl.BlockSpec((1, pair, 1, lon_count), lambda f, h: (f, h, 0, 0)),
            pl.BlockSpec((1, pair, 1, lon_count), lambda f, h: (f, h, 0, 0)),
            pl.BlockSpec((rows, lon_count), lambda f, h: (0, 0)),
        ],
        out_specs=pl.BlockSpec((rows, pair * lat_dev), lambda f, h: (0, f * halves + h)),
        out_shape=pltpu.HBM((rows, fields * lev_dev * lat_dev), jnp.bfloat16),
        compiler_params=pltpu.CompilerParams(vmem_limit_bytes=VMEM_BYTES),
        cost_estimate=pl.CostEstimate(
            flops=2 * rows * lon_count * fields * lev_dev * lat_dev,
            bytes_accessed=4 * rows * fields * lev_dev * lat_dev,
            transcendentals=0,
        ),
    )(x, x, before, after, table)


def legendre_kernel(
    dims, rates_ref, modes_ref, wave_ref, x_ref, basis_ref, *rest
):
    fields, levels, lev_dev, lev_count, subs, parts = dims
    rest = rest[-len(parts) - 3 :]
    spec_ref, y_refs, (flat_ref, work_ref) = rest[0], rest[1:-2], rest[-2:]
    group, wave_count, lat_count = basis_ref.shape
    cols = fields * 2 * levels
    tiles = lat_count // LANES
    wave_tiles = wave_count // LANES
    wide_count = x_ref.shape[0] // lev_count
    per_tile = lat_count // wide_count // LANES
    jw = LANES // levels

    def place(f, r, l):
        return (f * 2 + r) * levels + l

    for w in range(wide_count):
        for lx in range(lev_count):
            for f in range(fields):
                for l in range(lev_dev):
                    for p in range(per_tile):
                        lane = ((f * lev_dev + l) * per_tile + p) * LANES
                        for r in range(2):
                            block = x_ref[w * lev_count + lx, r, :, lane : lane + LANES].astype(jnp.float32)
                            start = place(f, r, lx * lev_dev + l)
                            for h in range(group // 8):
                                flat_ref[w * per_tile + p, pl.ds(start + h * 8 * cols, 8, stride=cols), :] = block[
                                    h * 8 : (h + 1) * 8
                                ]

    def forward(s, carry):
        rows = pl.ds(pl.multiple_of(s * cols, 8), cols)
        lhs = jnp.concatenate([flat_ref[t, rows, :].astype(jnp.bfloat16) for t in range(tiles)], axis=1)
        raw = lax.dot_general(
            lhs, basis_ref[s], (((1,), (1,)), ((), ())), preferred_element_type=jnp.float32
        )
        for t in range(wave_tiles):
            work_ref[t, rows, :] = raw[:, t * LANES : (t + 1) * LANES]
        return carry

    lax.fori_loop(0, group, forward, 0, unroll=16)

    def couple_tile(step, carry):
        t, h = lax.div(step, group // 8), lax.rem(step, group // 8)
        slot0 = pl.multiple_of(h * 8, 8)
        wave = wave_ref[pl.ds(slot0, 8), :]
        degree = wave + lax.broadcasted_iota(jnp.int32, (8, LANES), 1) + t * LANES
        inside = degree < wave_count
        curvature = (degree * (degree + 1)).astype(jnp.float32) * (1.0 / float(wave_count * wave_count))
        per_slot = fields * levels * wave_tiles * 2

        def gain(f, l):
            return jnp.where(inside, 1.0 / (1.0 + curvature * rates_ref[f, l]), 0.0)

        def where(f, r, l):
            return pl.ds(slot0 * cols + place(f, r, l), 8, stride=cols)

        def keep(f, r, l, value):
            work_ref[t, where(f, r, l), :] = value
            row = ((f * levels + l) * wave_tiles + t) * 2 + r
            spec_ref[pl.ds(slot0 * per_slot + row, 8, stride=per_slot), :] = value

        for l in range(levels):
            scale = gain(0, l)
            for r in range(2):
                keep(0, r, l, work_ref[t, where(0, r, l), :] * scale)
        for f in range(1, fields):
            raw = [[work_ref[t, where(f, r, l), :] for l in range(levels)] for r in range(2)]
            scaled = [[], []]
            for i in range(levels):
                totals = [raw[r][0] * modes_ref[0, i] for r in range(2)]
                for l in range(1, levels):
                    mode = modes_ref[l, i]
                    totals = [totals[r] + raw[r][l] * mode for r in range(2)]
                scale = gain(f, i)
                for r in range(2):
                    scaled[r].append(totals[r] * scale)
            for l in range(levels):
                totals = [scaled[r][0] * modes_ref[l, 0] for r in range(2)]
                for i in range(1, levels):
                    mode = modes_ref[l, i]
                    totals = [totals[r] + scaled[r][i] * mode for r in range(2)]
                for r in range(2):
                    keep(f, r, l, totals[r])
        return carry

    lax.fori_loop(0, wave_tiles * (group // 8), couple_tile, 0)

    def backward(s, carry):
        rows = pl.ds(pl.multiple_of(s * cols, 8), cols)
        lhs = jnp.concatenate(
            [work_ref[t, rows, :].astype(jnp.bfloat16) for t in range(wave_tiles)], axis=1
        )
        back = jnp.dot(lhs, basis_ref[s], preferred_element_type=jnp.float32)
        for t in range(tiles):
            flat_ref[t, rows, :] = back[:, t * LANES : (t + 1) * LANES]
        return carry

    lax.fori_loop(0, group, backward, 0, unroll=16)

    lane = lax.broadcasted_iota(jnp.int32, (8, LANES), 1)
    weights = [
        jnp.where(wave_ref[h * 8 : (h + 1) * 8, :] == 0, 1.0, 2.0) for h in range(group // 8)
    ]
    part_of = {}
    for index, members in enumerate(parts):
        for place_in, sub in enumerate(members):
            part_of[sub] = (index, place_in)
    dest_per_tile = levels // subs if levels >= subs else 1

    def scatter(t, carry):
        for f in range(fields):
            for r in range(2):
                halves = []
                for h in range(group // 8):
                    start = h * 8 * cols
                    pieces = [
                        flat_ref[t, pl.ds(start + place(f, r, l), 8, stride=cols), :] * weights[h]
                        for l in range(levels)
                    ]
                    bit = 1
                    while bit < levels:
                        shift = bit * jw
                        odd = (lane // shift) % 2 == 1
                        swapped = list(pieces)
                        for l in range(levels):
                            if l & bit == 0:
                                low, high = pieces[l], pieces[l | bit]
                                swapped[l] = jnp.where(odd, pltpu.roll(high, shift, 1), low)
                                swapped[l | bit] = jnp.where(odd, high, pltpu.roll(low, LANES - shift, 1))
                        pieces = swapped
                        bit *= 2
                    halves.append(pieces)
                for g in range(levels):
                    block = jnp.concatenate([half[g] for half in halves], axis=0).astype(jnp.bfloat16)
                    index, place_in = part_of[g % subs]
                    y_refs[index][t * dest_per_tile + g // subs, 0, place_in, f, r] = block
        return carry

    lax.fori_loop(0, tiles, scatter, 0)


def legendre(received, lat_basis, wave_part, vert_modes, vert_rates, chunk, so_far, dims):
    fields, levels, lev_dev, lev_count, subs, parts, chunks = dims
    devices = received.shape[0]
    slots, wave_count, lat_count = lat_basis.shape
    group = PACK
    lanes_in = received.shape[-1]
    here = slots // chunks
    steps = here // group
    cols = fields * 2 * levels
    per_slot = fields * levels * (wave_count // LANES) * 2
    args = [vert_rates, vert_modes, wave_part[:, None], received.reshape(devices, 2, here, lanes_in), lat_basis]
    aliases = {}
    if so_far is not None:
        kept = [0] + list(range(2, 1 + len(parts)))
        aliases = {len(args) + n: k for n, k in enumerate(kept)}
        args = args + [so_far[k] for k in kept]
    first = chunk * steps

    def part_spec(index, part):
        block = (devices, 1, len(part), fields, 2, group, LANES)
        if index == 0:
            return pl.BlockSpec(block, lambda g: (0, 0, 0, 0, 0, g, 0))
        return pl.BlockSpec(block, lambda g: (0, chunk, 0, 0, 0, g, 0))

    return pl.pallas_call(
        functools.partial(legendre_kernel, (fields, levels, lev_dev, lev_count, subs, parts)),
        grid=(steps,),
        in_specs=[
            pl.BlockSpec(memory_space=pltpu.SMEM),
            pl.BlockSpec(memory_space=pltpu.SMEM),
            pl.BlockSpec((group, 1), lambda g: (first + g, 0)),
            pl.BlockSpec((devices, 2, group, lanes_in), lambda g: (0, 0, g, 0)),
            pl.BlockSpec((group, wave_count, lat_count), lambda g: (first + g, 0, 0)),
        ]
        + [pl.BlockSpec(memory_space=pl.ANY)] * len(aliases),
        out_specs=[pl.BlockSpec((group * per_slot, LANES), lambda g: (first + g, 0))]
        + [part_spec(i, p) for i, p in enumerate(parts)],
        out_shape=[pltpu.HBM((slots * per_slot, LANES), jnp.float32)]
        + [
            pltpu.HBM(
                (devices, chunks if i else 1, len(p), fields, 2, here, LANES), jnp.bfloat16
            )
            for i, p in enumerate(parts)
        ],
        input_output_aliases=aliases,
        scratch_shapes=[
            pltpu.VMEM((lat_count // LANES, group * cols, LANES), jnp.float32),
            pltpu.VMEM((wave_count // LANES, group * cols, LANES), jnp.float32),
        ],
        compiler_params=pltpu.CompilerParams(vmem_limit_bytes=VMEM_BYTES),
        cost_estimate=pl.CostEstimate(
            flops=40 * here * cols * wave_count * lat_count,
            bytes_accessed=2 * here * wave_count * lat_count,
            transcendentals=0,
        ),
    )(*args)


def column_kernel(
    shape, scalars_ref, weights_ref, *rest
):
    fields, levels, jw, padded, bands, chunks, count = shape
    table_refs, y_refs = rest[:chunks], rest[chunks : chunks + count]
    out_ref, grid_ref, done_ref, gain_ref = rest[-4:]
    features = fields * levels
    for i in range(features):
        gain_ref[i : i + 1, :] = jnp.full((1, LANES), scalars_ref[i])
    subs = y_refs[0].shape[2]
    lon_count = table_refs[0].shape[1]
    lon_tiles = lon_count // LANES
    row = lax.rem(lax.broadcasted_iota(jnp.int32, (3 * bands, lon_count), 0), bands).astype(jnp.float32)
    units = weights_ref.shape[0] - padded
    entry_cols = slice(units, units + padded + 3 * bands)
    gain = jnp.concatenate([gain_ref[...]] * lon_tiles, axis=1)
    for sub in range(subs):
        pieces = [(y_ref, c) for y_ref in y_refs for c in range(y_ref.shape[1])]
        grid_mid = 0.0
        for (y_ref, c), table_ref in zip(pieces, table_refs):
            lhs = jnp.concatenate([y_ref[:, c, sub, f].reshape(-1, LANES) for f in range(fields)], axis=1)
            grid_mid = grid_mid + lax.dot_general(
                lhs, table_ref[...], (((0,), (0,)), ((), ())), preferred_element_type=jnp.float32
            )
        grid_mid = grid_mid.astype(jnp.bfloat16).astype(jnp.float32)
        for t in range(lon_tiles):
            grid_ref[t] = grid_mid[:, t * LANES : (t + 1) * LANES]

        def one_row(j, carry):
            where = pl.ds(j, features, stride=jw)
            x = jnp.concatenate([grid_ref[t, where, :] for t in range(lon_tiles)], axis=1)
            mean = jnp.sum(x * x, axis=0, keepdims=True) * (1.0 / features)
            normed = x * lax.rsqrt(mean + norm_eps) * gain
            if padded > features:
                normed = jnp.concatenate(
                    [normed, jnp.zeros((padded - features, lon_count), jnp.float32)], axis=0
                )
            chosen = row == scalars_ref[features + sub * jw + j]
            entries = jnp.concatenate(
                [normed.astype(jnp.bfloat16), jnp.where(chosen, 1.0, 0.0).astype(jnp.bfloat16)], axis=0
            )
            half = jnp.dot(weights_ref[:units, entry_cols], entries, preferred_element_type=jnp.float32)
            hidden = (half * jnp.tanh(half) + half).astype(jnp.bfloat16)
            half = jnp.dot(weights_ref[:units, :units], hidden, preferred_element_type=jnp.float32)
            hidden = (half * jnp.tanh(half) + half).astype(jnp.bfloat16)
            grown = jnp.dot(weights_ref[units:, :units], hidden, preferred_element_type=jnp.float32)
            result = x + grown[:features]
            for t in range(lon_tiles):
                done_ref[t, where, :] = result[:, t * LANES : (t + 1) * LANES]
            return carry

        lax.fori_loop(0, jw, one_row, 0, unroll=4)
        for t in range(lon_tiles):
            out_ref[:, sub * jw : (sub + 1) * jw, t * LANES : (t + 1) * LANES] = (
                done_ref[t].reshape(features, jw, LANES).astype(jnp.bfloat16)
            )


def column_part(arrived, tables, bands_here, weights, so_far, first, lat_quarter, dims):
    fields, levels, jw = dims
    w_all, gain, padded, bands = weights
    units = w_all.shape[0] - padded
    scalars = jnp.concatenate([gain, bands_here.astype(jnp.float32)])
    subs = arrived[0].shape[2]
    features = fields * levels
    depth, lon_count = sum(t.shape[0] for t in tables), tables[0].shape[1]
    rows = subs * jw
    whole = pl.BlockSpec(memory_space=pltpu.VMEM)
    args = [scalars, w_all] + list(tables) + list(arrived)
    specs = [pl.BlockSpec(memory_space=pltpu.SMEM)] + [whole] * (len(args) - 1)
    aliases = {}
    if so_far is not None:
        args.append(so_far)
        specs.append(pl.BlockSpec(memory_space=pl.ANY))
        aliases = {len(args) - 1: 0}
    block = first // rows
    return pl.pallas_call(
        functools.partial(column_kernel, (fields, levels, jw, padded, bands, len(tables), len(arrived))),
        grid=(1,),
        in_specs=specs,
        out_specs=pl.BlockSpec((features, rows, lon_count), lambda g: (0, block, 0)),
        out_shape=jax.ShapeDtypeStruct((features, lat_quarter, lon_count), jnp.bfloat16),
        input_output_aliases=aliases,
        scratch_shapes=[
            pltpu.VMEM((lon_count // LANES, features * jw, LANES), jnp.float32),
            pltpu.VMEM((lon_count // LANES, features * jw, LANES), jnp.float32),
            pltpu.VMEM((features, LANES), jnp.float32),
        ],
        compiler_params=pltpu.CompilerParams(vmem_limit_bytes=VMEM_BYTES),
        cost_estimate=pl.CostEstimate(
            flops=2 * rows * lon_count * units * (units + 2 * 256) + 2 * depth * lon_count * features * rows,
            bytes_accessed=4 * features * rows * lon_count,
            transcendentals=2 * rows * lon_count * units,
        ),
    )(*args)


def local_tiled(
    grid_state, wave_slots, lat_basis, vert_modes, vert_rates, band_sizes, norm_gain, w_in, band_bias, w_mid, w_out
):
    _, fields, lev_dev, lat_dev, lon_count = grid_state.shape
    wide_count = lax.axis_size("wide")
    lev_count = lax.axis_size("lev")
    devices = wide_count * lev_count
    slot_dev, wave_count, lat_count = lat_basis.shape
    levels = lev_dev * lev_count
    lat_quarter = lat_count // devices
    jw = LANES // levels
    subs = lat_quarter // jw
    block_index = lax.axis_index("wide") * lev_count + lax.axis_index("lev")

    chunks = 2 if slot_dev % (2 * PACK) == 0 else 1
    angles = angle_parts(wave_slots, lon_count)
    edges = (grid_state[:, :, :, lat_dev - 1 :], grid_state[:, :, :, :1])
    up = [(i, i + 1) for i in range(wide_count - 1)]
    down = [(j, i) for i, j in up]
    before = lax.ppermute(edges[0], "wide", up)
    after = lax.ppermute(edges[1], "wide", down)
    tables = [table_of(angles, devices, lon_count, c, chunks) for c in range(chunks)]

    def exchange(parcel):
        return lax.all_to_all(parcel, ("wide", "lev"), split_axis=0, concat_axis=0, tiled=True)

    coeffs = [fourier(grid_state, before, after, table) for table in tables]
    received = [exchange(c.reshape(devices, -1, c.shape[1])) for c in coeffs]
    wave_part = lax.dynamic_slice_in_dim(wave_slots, block_index * slot_dev, slot_dev)
    count = 2 if subs % 2 == 0 else 1
    parts = tuple(
        tuple(range(i * subs // count, (i + 1) * subs // count)) for i in range(count)
    )
    dims = (fields, levels, lev_dev, lev_count, subs, parts, chunks)
    bands = band_sizes.shape[0]
    latitude = block_index * lat_quarter + jnp.arange(lat_quarter, dtype=jnp.int32)
    bands_here = jnp.sum(
        (latitude[:, None] >= jnp.cumsum(band_sizes)[None, :]).astype(jnp.int32), axis=1
    )
    features = fields * levels
    padded = -(-features // PACK) * PACK
    pieces, rest = [], band_bias
    for _ in range(3):
        piece = lax.reduce_precision(rest, 8, 7)
        pieces.append(piece.astype(jnp.bfloat16))
        rest = rest - piece
    half = jnp.bfloat16(0.5)
    w_first = jnp.concatenate(
        [jnp.pad(w_in, ((0, 0), (0, padded - features)))] + pieces, axis=1
    ) * half
    units = w_mid.shape[0]
    w_all = jnp.zeros((units + padded, units + -(-w_first.shape[1] // LANES) * LANES), jnp.bfloat16)
    w_all = w_all.at[:units, :units].set(w_mid * half)
    w_all = w_all.at[units : units + features, :units].set(w_out)
    w_all = w_all.at[:units, units : units + w_first.shape[1]].set(w_first)
    received[0], w_all, bands_here = lax.optimization_barrier((received[0], w_all, bands_here))
    weights = (w_all, norm_gain, padded, bands)
    so_far, arrived_first = None, []
    for c in range(chunks):
        so_far = legendre(received[c], lat_basis, wave_part, vert_modes, vert_rates, c, so_far, dims)
        parcel = so_far[1]
        if arrived_first:
            arrived_first[-1], parcel = lax.optimization_barrier((arrived_first[-1], parcel))
        arrived_first.append(exchange(parcel))
    spectral = so_far[0].reshape(slot_dev, fields, levels, wave_count // LANES, 2, LANES)
    spectral = spectral.transpose(0, 1, 2, 4, 3, 5).reshape(slot_dev, 1, fields, levels, 2, wave_count)

    new_state = None
    for index, part in enumerate(parts):
        arrived = [exchange(so_far[1 + index])] if index else arrived_first
        rows = slice(part[0] * jw, (part[-1] + 1) * jw)
        new_state = column_part(
            arrived, tables, bands_here[rows], weights, new_state, part[0] * jw, lat_quarter, (fields, levels, jw)
        )
    return spectral, new_state.reshape(1, fields, levels, lat_quarter, lon_count)


def local(grid_state, wave_slots, lat_basis, *rest):
    members, _, lev_dev, lat_dev, lon_count = grid_state.shape
    lev_count = lax.axis_size("lev")
    slot_dev, wave_count, lat_count = lat_basis.shape
    levels = lev_dev * lev_count
    lat_quarter = lat_dev // lev_count
    fits = (
        members == 1
        and levels == 8
        and lat_dev % LANES == 0
        and lon_count % LANES == 0
        and wave_count % LANES == 0
        and slot_dev % PACK == 0
        and lat_quarter % (LANES // levels) == 0
        and lat_quarter <= LANES
    )
    chosen = local_tiled if fits else local_plain
    return chosen(grid_state, wave_slots, lat_basis, *rest)


def solution(mesh):
    placed = (
        P(("groups", "fld"), None, "lev", "wide", None),
        P(),
        P(("wide", "lev"), None, None),
        P(),
        P(),
        P(),
        P(),
        P(),
        P(),
        P(),
        P(),
    )
    return jax.shard_map(
        local,
        mesh=mesh,
        in_specs=placed,
        out_specs=(
            P(("wide", "lev"), ("groups", "fld"), None, None, None, None),
            P(("groups", "fld"), None, None, ("wide", "lev"), None),
        ),
        check_vma=False,
    )
```
